128 devices in a mesh: seq: 16 (over z_hi, y, core), tp: 8 (over x, z_lo).
Axes of the slice: x: 4, y: 4, z: 4 (z_hi: 2, z_lo: 2; z = z_hi * 2 + z_lo), core: 2. Of those that a mesh axis runs over, the one named last changes fastest.
Arguments:
- temporal_out: bfloat16 [16384, 4096], P('seq', 'tp'), may hold values from -6 to 6
- context_weight: bfloat16 [4096, 1024], P('tp'), may hold values from -0.125 to 0.125
- text_ids: int32 [16384], P('seq'), may hold values from 0 to 16383
- code_ids: int32 [16384, 7], P('seq'), may hold values from 0 to 2047
- text_table: bfloat16 [16384, 1024], P(None, 'tp'), may hold values from -40 to 40
- code_tables: bfloat16 [7, 2048, 1024], P(None, None, 'tp'), may hold values from -40 to 40
- norm_gain: float32 [1024], replicated, may hold values from 0.5 to 1.5
- gate_weight: bfloat16 [1024, 2048], replicated, may hold values from -0.1875 to 0.1875
- up_weight: bfloat16 [1024, 2048], replicated, may hold values from -0.1875 to 0.1875
- hidden_grad: bfloat16 [16384, 8, 2048], P(('seq', 'tp')), may hold values from -0.75 to 0.75
- stream_grad: bfloat16 [16384, 8, 1024], P(('seq', 'tp')), may hold values from -0.75 to 0.75
Outputs:
- gate_grad: float32 [1024, 2048], P(('seq', 'tp'))
- up_grad: float32 [1024, 2048], P(('seq', 'tp'))
- gain_grad: float32 [1024], P(('seq', 'tp'))
- text_grad: float32 [16384, 1024], P('seq', 'tp')
- code_grad: float32 [7, 2048, 1024], P(None, 'seq', 'tp')
- context_grad: bfloat16 [16384, 1024], P(('seq', 'tp'))
The draws below stay inside these ranges and needn't reach their ends.
All inputs are finite; a program needn't handle non-finite values.
Results may differ from the reference program's by a relative error of at most 0.04.
Values may be sent and summed in bfloat16 or wider, within the bound.
A program may use at most 128 MiB of HBM per device.

```python
import math
import jax
import jax.numpy as jnp
import numpy as np
from jax import lax

D = 4096
DD = 1024
FF = 2048
TV = 16384
CARD = 2048
STEPS = 8
CODES = 7
FR_DEV = 128
FRAMES = 16384
N_SEQ = 16
N_TP = 8


def table_values(key, row_count, col_count, log_reach):
    key_rows, key_cols, key_normal = jax.random.split(key, 3)
    row_scale = jnp.exp(jax.random.uniform(key_rows, (row_count, 1), jnp.float32, -log_reach, log_reach))
    col_scale = jnp.exp(jax.random.uniform(key_cols, (1, col_count), jnp.float32, -log_reach, log_reach))
    normal_part = jax.random.truncated_normal(key_normal, -4.0, 4.0, (row_count, col_count), jnp.float32)
    mixture = normal_part
    return mixture * row_scale * col_scale


def draw_text_table(key, part):
    key = jax.random.fold_in(key, 11)
    values = table_values(key, TV, DD, 1.15)
    return values.astype(jnp.bfloat16)


def draw_code_tables(key, part):
    key = jax.random.fold_in(key, 12)
    values = table_values(key, CODES * CARD, DD, 1.15)
    return values.reshape(CODES, CARD, DD).astype(jnp.bfloat16)


def with_ends(drawn, rng, low, largest):
    longest = drawn.shape.index(max(drawn.shape))
    spots = []
    for shift in (0, 1):
        where = [jax.random.randint(jax.random.fold_in(rng, axis), (), 0, length) for axis, length in enumerate(drawn.shape)]
        where[longest] = (where[longest] + shift) % drawn.shape[longest]
        spots.append(tuple(where))
    return drawn.at[spots[0]].set(low).at[spots[1]].set(largest)


def spiked(drawn, own_key, source, target, shards_of, factor):
    owner, partner = [(jnp.arange(drawn.shape[position]) // (drawn.shape[position] // shards_of)).reshape([-1 if axis == position else 1 for axis in range(drawn.ndim)]) for position in (source, target)]
    chosen = jax.random.permutation(own_key, shards_of)[partner]
    strong = (owner == chosen) | (owner == (partner + shards_of // 2) % shards_of)
    return jnp.where(strong, factor * drawn, drawn)


def levels(key, dims, shards, low, high):
    factor_of = 1.0
    for dim, blocks in shards:
        heights = jax.random.uniform(jax.random.fold_in(jax.random.fold_in(key, 6), dim), (blocks,), jnp.float32, low / len(shards), high / len(shards))
        factor_of = factor_of * jnp.repeat(jnp.exp(heights), dims[dim] // blocks).reshape((-1,) + (1,) * (len(dims) - 1 - dim))
    return factor_of


def cumulative_ranks(amount, slope):
    portions = [(1 << 20) // math.isqrt(standing ** slope) + 1 for standing in range(1, amount + 1)]
    deviation = 1 + sum(portions) // (1 << 30)
    return np.cumsum(np.array([max(1, weight // deviation) for weight in portions]))


def skewed_ids(key, shape, amount, skew):
    listing = cumulative_ranks(amount, skew)
    pick = jax.random.randint(jax.random.fold_in(key, 1), shape, 0, int(listing[amount - 1]))
    rank = jnp.searchsorted(jnp.asarray(listing, jnp.int32), pick, side="right")
    return jax.random.permutation(jax.random.fold_in(key, 2), amount)[rank].astype(jnp.int32)


def scatter_about(rng, dims, width, limit, cuts=(), kind=jnp.bfloat16):
    gain = levels(rng, dims, cuts, -0.22, 0.18) if cuts else 1.0
    drawn = jax.random.normal(rng, dims, jnp.float32) * width * gain
    return jnp.minimum(jnp.maximum(drawn, -limit), limit).astype(kind)


def noise_with(own_key, shape, scale, reach, pieces, heavy, kind=jnp.bfloat16):
    array = scale * jax.random.normal(own_key, shape, jnp.float32)
    if pieces:
        array = array * levels(own_key, shape, pieces, -0.22, 0.18)
    return jnp.clip(spiked(array, jax.random.fold_in(own_key, 3), *heavy), -reach, reach).astype(kind)


def setup_inputs(seed: int = 0) -> dict:
    key_of = jax.random.split(jax.random.key(seed), 12)
    temporal_out = scatter_about(key_of[0], (FRAMES, D), 1.0, 6.0, ((0, 16), (1, 8)))
    context_weight = noise_with(key_of[1], (D, DD), D ** -0.5, 0.125, ((0, 8),), (0, 1, 8, 2.0))
    text_ids = with_ends(skewed_ids(key_of[2], (FRAMES,), TV, 2), jax.random.fold_in(key_of[2], 3), 0, TV - 1).astype(jnp.int32)
    code_ids = with_ends(skewed_ids(key_of[3], (FRAMES, CODES), CARD, 1), jax.random.fold_in(key_of[3], 3), 0, CARD - 1).astype(jnp.int32)
    text_table = draw_text_table(jax.random.fold_in(key_of[11], 71), 0)
    code_tables = draw_code_tables(jax.random.fold_in(key_of[11], 71), 0)
    norm_gain = jnp.clip(1.0 + 0.1 * jax.random.normal(key_of[6], (DD,), jnp.float32), 0.5, 1.5)
    gate_weight = scatter_about(key_of[7], (DD, FF), DD ** -0.5, 0.1875)
    up_weight = scatter_about(key_of[8], (DD, FF), DD ** -0.5, 0.1875)
    hidden_grad = scatter_about(key_of[9], (FRAMES, STEPS, FF), 0.125, 0.75, ((0, 128),))
    stream_grad = scatter_about(key_of[10], (FRAMES, STEPS, DD), 0.125, 0.75, ((0, 128),))
    return dict(temporal_out=temporal_out, context_weight=context_weight, text_ids=text_ids, code_ids=code_ids, text_table=text_table, code_tables=code_tables, norm_gain=norm_gain, gate_weight=gate_weight, up_weight=up_weight, hidden_grad=hidden_grad, stream_grad=stream_grad)


EPSILON = 1e-05

def through_bfloat(values):
    return lax.optimization_barrier(values.astype(jnp.bfloat16)).astype(jnp.float32)

def reference(temporal_out, context_weight, text_ids, code_ids, text_table, code_tables, norm_gain, gate_weight, up_weight, hidden_grad, stream_grad):
    seq_frames = FR_DEV * N_TP
    block_width = D // N_TP
    code_offsets = jnp.arange(CODES, dtype=jnp.int32)[None, :] * CARD
    flat_codes = code_tables.reshape(CODES * CARD, DD)
    gain_row = norm_gain.astype(jnp.float32)
    over_rows = (((0,), (0,)), ((), ()))
    transposed = (((1,), (1,)), ((), ()))

    def shard_step(totals, shard_index):
        gate_total, up_total, gain_total, text_total, code_total = totals
        first_frame = (shard_index * seq_frames).astype(jnp.int32)
        features = lax.dynamic_slice_in_dim(temporal_out, first_frame, seq_frames, 0)
        text_block = lax.dynamic_slice_in_dim(text_ids, first_frame, seq_frames, 0)
        code_block = lax.dynamic_slice_in_dim(code_ids, first_frame, seq_frames, 0)
        cotangent = lax.dynamic_slice_in_dim(hidden_grad, first_frame, seq_frames, 0)
        stream = lax.dynamic_slice_in_dim(stream_grad, first_frame, seq_frames, 0)
        context = jnp.zeros((seq_frames, DD), jnp.float32)
        for tp_block in range(N_TP):
            lower = tp_block * block_width
            upper = lower + block_width
            partial_value = jnp.dot(features[:, lower:upper], context_weight[lower:upper], preferred_element_type=jnp.float32)
            context = context + through_bfloat(partial_value)
        text_rows = jnp.take(text_table, text_block, axis=0)
        code_rows = jnp.take(flat_codes, code_block + code_offsets, axis=0)
        embedded = jnp.concatenate([text_rows[:, None, :], code_rows], axis=1)
        depth_in = through_bfloat(context[:, None, :] + embedded.astype(jnp.float32))
        depth_rows = depth_in.reshape(seq_frames * STEPS, DD)
        inv_rms = lax.rsqrt(lax.optimization_barrier(jnp.mean(depth_rows * depth_rows, axis=1, keepdims=True)) + EPSILON)
        unit_rows = depth_rows * inv_rms
        normed = (unit_rows * gain_row).astype(jnp.bfloat16)
        gate_values = jnp.dot(normed, gate_weight, preferred_element_type=jnp.float32)
        up_values = jnp.dot(normed, up_weight, preferred_element_type=jnp.float32)
        gate_sigmoid = jax.nn.sigmoid(gate_values)
        upstream = cotangent.reshape(seq_frames * STEPS, FF).astype(jnp.float32)
        gate_back = (upstream * up_values * gate_sigmoid * (1.0 + gate_values * (1.0 - gate_sigmoid))).astype(jnp.bfloat16)
        up_back = (upstream * gate_values * gate_sigmoid).astype(jnp.bfloat16)
        normed_back = lax.dot_general(gate_back, gate_weight, transposed, preferred_element_type=jnp.float32)
        normed_back = normed_back + lax.dot_general(up_back, up_weight, transposed, preferred_element_type=jnp.float32)
        gain_part = lax.optimization_barrier(jnp.sum(normed_back * unit_rows, axis=0))
        scaled_back = normed_back * gain_row
        stream_rows = stream.reshape(seq_frames * STEPS, DD).astype(jnp.float32)
        depth_back = stream_rows + inv_rms * (scaled_back - unit_rows * lax.optimization_barrier(jnp.mean(scaled_back * unit_rows, axis=1, keepdims=True)))
        depth_grid = through_bfloat(depth_back).reshape(seq_frames, STEPS, DD)
        context_back = lax.optimization_barrier(jnp.sum(depth_grid, axis=1)).astype(jnp.bfloat16)
        gate_total = gate_total + lax.dot_general(normed, gate_back, over_rows, preferred_element_type=jnp.float32)
        up_total = up_total + lax.dot_general(normed, up_back, over_rows, preferred_element_type=jnp.float32)
        gain_total = gain_total + gain_part
        text_part = jax.ops.segment_sum(depth_grid[:, 0], text_block, num_segments=TV)
        code_part = jax.ops.segment_sum(depth_grid[:, 1:].reshape(seq_frames * CODES, DD), (code_block + code_offsets).reshape(-1), num_segments=CODES * CARD)
        text_total = text_total + through_bfloat(text_part)
        code_total = code_total + through_bfloat(code_part)
        return ((gate_total, up_total, gain_total, text_total, code_total), context_back)
    initial = (jnp.zeros((DD, FF), jnp.float32), jnp.zeros((DD, FF), jnp.float32), jnp.zeros((DD,), jnp.float32), jnp.zeros((TV, DD), jnp.float32), jnp.zeros((CODES * CARD, DD), jnp.float32))
    totals, context_blocks = lax.scan(shard_step, initial, jnp.arange(N_SEQ, dtype=jnp.int32))
    gate_grad, up_grad, gain_grad, text_grad, code_total = totals
    return (gate_grad, up_grad, gain_grad, text_grad, code_total.reshape(CODES, CARD, DD), context_blocks.reshape(FRAMES, DD))
```

```python
import functools

import jax
import jax.numpy as jnp
from jax import lax
from jax.experimental import pallas as pl
from jax.experimental.pallas import tpu as pltpu
from jax.sharding import PartitionSpec as P

EPSILON = 1e-05

MESH = pl.DeviceIdType.MESH
F32 = jnp.float32
BF16 = jnp.bfloat16
VMEM_LIMIT = 60 * 1024 * 1024


def position():
    seq = lax.axis_index("seq")
    tp = lax.axis_index("tp")
    core = lax.rem(seq, 2)
    y = lax.rem(lax.div(seq, 2), 4)
    z_hi = lax.div(seq, 8)
    x = lax.div(tp, 2)
    z_lo = lax.rem(tp, 2)
    return core, x, y, z_hi * 2 + z_lo


def device_at(core, x, y, z):
    seq = (lax.div(z, 2) * 4 + y) * 2 + core
    tp = x * 2 + lax.rem(z, 2)
    return (seq, tp)


def step_to(value, by):
    return lax.rem(value + by, 4)


def greet(devices):
    barrier = pltpu.get_barrier_semaphore()
    for device in devices:
        pl.semaphore_signal(barrier, inc=1, device_id=device, device_id_type=MESH)
    pl.semaphore_wait(barrier, len(devices))


def add_blocks(count, target, sources):
    def body(i, carry):
        total = sources[0](i)[...].astype(F32)
        for source in sources[1:]:
            total = total + source(i)[...].astype(F32)
        ref = target(i)
        ref[...] = total.astype(ref.dtype)
        return carry

    lax.fori_loop(0, count, body, 0)


class Copies:
    def __init__(self, send_sems, recv_sems):
        self.send_sems, self.recv_sems, self.made = send_sems, recv_sems, []

    def send(self, source, target, device):
        at = len(self.made)
        copy = pltpu.make_async_remote_copy(
            src_ref=source,
            dst_ref=target,
            send_sem=self.send_sems.at[at],
            recv_sem=self.recv_sems.at[at],
            device_id=device,
            device_id_type=MESH,
        )
        copy.start()
        self.made.append(copy)
        return copy

    def finish(self):
        for copy in self.made:
            copy.wait_send()


class Ring:
    def __init__(self, copies, here, device, part, pass_on, direct, ended):
        self.copies, self.here, self.device, self.part = copies, here, device, part
        self.pass_on, self.direct, self.ended = pass_on, direct, ended

    def first(self):
        up, down, far = (step_to(self.here, by) for by in (1, 3, 2))
        up_device, down_device = self.device(up), self.device(down)
        send = self.copies.send
        self.from_down = send(self.part(far, 0), self.pass_on(0), up_device)
        self.from_up = send(self.part(far, 1), self.pass_on(1), down_device)
        self.near = [
            send(self.part(up, 1), self.direct(1), up_device),
            send(self.part(down, 0), self.direct(0), down_device),
        ]

    def second(self, add):
        up, down = step_to(self.here, 1), step_to(self.here, 3)
        self.from_down.wait_recv()
        add(self.part(up, 0), [self.part(up, 0), self.pass_on(0)])
        last_up = self.copies.send(self.part(up, 0), self.ended(0), self.device(up))
        self.from_up.wait_recv()
        add(self.part(down, 1), [self.part(down, 1), self.pass_on(1)])
        last_down = self.copies.send(self.part(down, 1), self.ended(1), self.device(down))
        self.last = [last_up, last_down]

    def third(self, add, out):
        for copy in self.near + self.last:
            copy.wait_recv()
        for half in (0, 1):
            add(out(half), [self.part(self.here, half), self.direct(half), self.ended(half)])


def reduce_kernel(
    normed, gate_back, up_back, gain, tables,
    gate_out, up_out, gain_out, text_out, code_out,
    turned, term, pair, x_pass, x_direct, x_ended, z_term, z_pass, z_direct, z_ended,
    y_term, y_pass, y_direct, y_ended, own, other, t_pass, t_direct, t_ended, t_sum, t_last,
    gain_own, gain_in, local_sem, send_sems, recv_sems,
):
    core, x, y, z = position()
    half_width = term.shape[-1] // 2
    text_rows = text_out.shape[0]
    table_rows = own.shape[2]
    half_rows = table_rows // 2
    z_hi = lax.div(z, 2)
    sibling = device_at(1 - core, x, y, z)
    x_device = lambda at: device_at(core, at, y, z)
    y_device = lambda at: device_at(core, x, at, z)
    z_device = lambda at: device_at(core, x, y, at)
    greet(
        [sibling]
        + [x_device(step_to(x, by)) for by in (1, 2, 3)]
        + [y_device(step_to(y, by)) for by in (1, 2, 3)]
        + [z_device(step_to(z, by)) for by in (1, 2, 3)]
    )
    copies = Copies(send_sems, recv_sems)
    halves = lambda half: pl.ds(half * half_width, half_width)

    keep = pltpu.make_async_copy(tables.at[core], own, local_sem)
    keep.start()
    table_pairs = [
        copies.send(tables.at[1 - core, i], other.at[i], sibling) for i in range(4)
    ]
    gain_own[0] = gain[...]
    gain_copy = copies.send(gain_own.at[0], gain_in.at[0], sibling)

    def make_term(q):
        turned[...] = normed[:, q * 256 : (q + 1) * 256].T

        def body(i, carry):
            columns = pl.ds(pl.multiple_of(i * 256, 256), 256)
            left = turned[...]
            gate = jnp.dot(left, gate_back[:, columns], preferred_element_type=F32)
            up = jnp.dot(left, up_back[:, columns], preferred_element_type=F32)
            both = jnp.concatenate([gate.reshape(32, 8, 256), up.reshape(32, 8, 256)], axis=1)
            both = both.astype(BF16).reshape(2, 2, 4, 2, 16, 256)
            for low in range(2):
                term[:, :, q * 2 + low, :, :, columns] = both[low]
            return carry

        lax.fori_loop(0, gate_back.shape[1] // 256, body, 0)

    pair_copies = []

    def send_pair(q):
        rows = pl.ds(q * 2, 2)
        pair_copies.append(copies.send(term.at[1 - core, :, rows], pair.at[:, rows], sibling))

    def add_pair(q):
        pair_copies[q].wait_recv()

        def body(i, carry):
            column, rest = lax.div(i, 4), lax.rem(i, 4)
            row, low = q * 2 + lax.div(rest, 2), lax.rem(rest, 2)
            here = term[core, column, row, low].astype(F32)
            term[core, column, row, low] = (here + pair[column, row, low].astype(F32)).astype(BF16)
            return carry

        lax.fori_loop(0, 16, body, 0)

    def add_four(out, refs):
        def body(i, carry):
            row, low = lax.div(i, 2), lax.rem(i, 2)
            total = refs[0][row, low].astype(F32)
            for ref in refs[1:]:
                total = total + ref[row, low].astype(F32)
            out[row, low] = total.astype(BF16)
            return carry

        lax.fori_loop(0, 4, body, 0)

    def x_ring(q):
        rows = pl.ds(q * 2, 2)
        pick = lambda ref: lambda half: ref.at[rows, :, :, halves(half)]
        return Ring(
            copies, x, x_device,
            lambda at, half: term.at[core, at, rows, :, :, halves(half)],
            pick(x_pass), pick(x_direct), pick(x_ended),
        )

    x_rings = [x_ring(q) for q in range(4)]

    def x_out(q):
        def finish(out, refs):
            def body(i, carry):
                row, low = lax.div(i, 2), lax.rem(i, 2)
                total = refs[0][row, low].astype(F32)
                for ref in refs[1:]:
                    total = total + ref[row, low].astype(F32)
                z_term[q // 2 * 2 + low, q % 2 * 2 + row, :, out] = total.astype(BF16)
                return carry

            lax.fori_loop(0, 4, body, 0)

        x_rings[q].third(finish, halves)

    t_half = lambda half: pl.ds(half * half_rows, half_rows)
    t_pick = lambda ref: lambda half: ref.at[:, t_half(half)]
    t_ring = Ring(
        copies, y, y_device,
        lambda at, half: own.at[at, :, t_half(half)],
        t_pick(t_pass), t_pick(t_direct), t_pick(t_ended),
    )

    def add_tables(out, refs):
        def body(i, carry):
            rows = pl.ds(pl.multiple_of(i * 64, 64), 64)
            for hi in range(2):
                total = refs[0][hi, rows].astype(F32)
                for ref in refs[1:]:
                    total = total + ref[hi, rows].astype(F32)
                out[hi, rows] = total.astype(BF16)
            return carry

        lax.fori_loop(0, half_rows // 64, body, 0)

    def pair_tables():
        keep.wait()
        for copy in table_pairs:
            copy.wait_recv()

        def body(i, carry):
            rows = pl.ds(pl.multiple_of(lax.rem(i, table_rows // 64) * 64, 64), 64)
            at = lax.div(i, table_rows // 64)
            for hi in range(2):
                total = own[at, hi, rows].astype(F32) + other[at, hi, rows].astype(F32)
                own[at, hi, rows] = total.astype(BF16)
            return carry

        lax.fori_loop(0, 4 * table_rows // 64, body, 0)

    def gain_round(index, device, here):
        gain_own[index] = gain_own[index - 1] + gain_sum
        return [
            copies.send(gain_own.at[index], gain_in.at[index * 3 + by - 3], device(step_to(here, by)))
            for by in (1, 2, 3)
        ]

    def gain_total(waited, slots):
        for copy in waited:
            copy.wait_recv()
        total = gain_in[slots[0]]
        for slot in slots[1:]:
            total = total + gain_in[slot]
        return total

    make_term(0)
    send_pair(0)
    pair_tables()
    t_ring.first()
    make_term(1)
    send_pair(1)
    add_pair(0)
    x_rings[0].first()
    gain_sum = gain_total([gain_copy], [0])
    gain_copies = gain_round(1, x_device, x)
    make_term(2)
    send_pair(2)
    add_pair(1)
    x_rings[1].first()
    t_ring.second(add_tables)
    make_term(3)
    send_pair(3)
    add_pair(2)
    x_rings[2].first()
    x_rings[0].second(add_four)
    add_pair(3)
    x_rings[3].first()
    x_rings[1].second(add_four)
    gain_sum = gain_total(gain_copies, [1, 2, 3])
    gain_copies = gain_round(2, y_device, y)
    x_out(0)
    x_rings[2].second(add_four)
    x_out(1)
    t_ring.third(add_tables, lambda half: t_sum.at[:, t_half(half)])
    t_copy = copies.send(t_sum.at[1 - z_hi], t_last, z_device(step_to(z, 2)))
    x_rings[3].second(add_four)
    x_out(2)
    gain_sum = gain_total(gain_copies, [4, 5, 6])
    gain_copies = gain_round(3, z_device, z)
    x_out(3)

    def add_few(out, refs):
        for i in range(4):
            total = refs[0][i].astype(F32)
            for ref in refs[1:]:
                total = total + ref[i].astype(F32)
            out[i] = total.astype(BF16)

    z_pick = lambda ref: lambda half: ref.at[:, :, halves(half)]
    z_ring = Ring(
        copies, z, z_device,
        lambda at, half: z_term.at[at, :, :, halves(half)],
        z_pick(z_pass), z_pick(z_direct), z_pick(z_ended),
    )
    z_ring.first()
    z_ring.second(add_few)
    z_ring.third(add_few, lambda half: y_term.at[:, :, halves(half)])

    def add_one(out, refs):
        total = refs[0][...].astype(F32)
        for ref in refs[1:]:
            total = total + ref[...].astype(F32)
        out[...] = total.astype(BF16)

    y_pick = lambda ref: lambda half: ref.at[:, halves(half)]
    y_ring = Ring(
        copies, y, y_device,
        lambda at, half: y_term.at[at, :, halves(half)],
        y_pick(y_pass), y_pick(y_direct), y_pick(y_ended),
    )
    y_ring.first()
    t_copy.wait_recv()

    def text_body(i, carry):
        rows = pl.ds(pl.multiple_of(i * 64, 64), 64)
        text_out[rows] = t_sum[z_hi, rows].astype(F32) + t_last[rows].astype(F32)
        return carry

    lax.fori_loop(0, text_rows // 64, text_body, 0)

    def code_body(i, carry):
        at = pl.ds(pl.multiple_of(i * 64, 64), 64)
        rows = pl.ds(pl.multiple_of(text_rows + i * 64, 64), 64)
        code_out[at] = t_sum[z_hi, rows].astype(F32) + t_last[rows].astype(F32)
        return carry

    lax.fori_loop(0, code_out.shape[0] // 64, code_body, 0)
    gain_out[...] = gain_own[3] + gain_total(gain_copies, [7, 8, 9])
    y_ring.second(add_one)

    def finish_weights(out, refs):
        total = refs[0][...].astype(F32)
        for ref in refs[1:]:
            total = total + ref[...].astype(F32)
        gate_out[:, out] = total[:8]
        up_out[:, out] = total[8:]

    y_ring.third(finish_weights, halves)
    copies.finish()


def reduce_all(normed, gate_back, up_back, gain_part, tables):
    features, width = normed.shape[1], gate_back.shape[1]
    table_rows = tables.shape[3]
    text_rows = table_rows * 8 // 15
    out_rows = features // 128
    bf = lambda *shape: pltpu.VMEM(shape, BF16)
    vmem = pl.BlockSpec(memory_space=pltpu.VMEM)
    return pl.pallas_call(
        reduce_kernel,
        out_shape=(
            jax.ShapeDtypeStruct((out_rows, width), F32),
            jax.ShapeDtypeStruct((out_rows, width), F32),
            jax.ShapeDtypeStruct((8, 128), F32),
            jax.ShapeDtypeStruct((text_rows, 128), F32),
            jax.ShapeDtypeStruct((table_rows - text_rows, 128), F32),
        ),
        in_specs=[vmem] * 4 + [pl.BlockSpec(memory_space=pl.ANY)],
        out_specs=(vmem,) * 5,
        scratch_shapes=[
            bf(256, normed.shape[0]),
            bf(2, 4, 8, 2, 16, width),
            bf(4, 8, 2, 16, width),
            bf(8, 2, 16, width), bf(8, 2, 16, width), bf(8, 2, 16, width),
            bf(4, 4, 16, width), bf(4, 16, width), bf(4, 16, width), bf(4, 16, width),
            bf(4, 16, width), bf(16, width), bf(16, width), bf(16, width),
            bf(4, 2, table_rows, 128), bf(4, 2, table_rows, 128),
            bf(2, table_rows, 128), bf(2, table_rows, 128), bf(2, table_rows, 128),
            bf(2, table_rows, 128), bf(table_rows, 128),
            pltpu.VMEM((4, 8, 128), F32), pltpu.VMEM((10, 8, 128), F32),
            pltpu.SemaphoreType.DMA,
            pltpu.SemaphoreType.DMA((64,)),
            pltpu.SemaphoreType.DMA((64,)),
        ],
        compiler_params=pltpu.CompilerParams(
            collective_id=1, has_side_effects=True, vmem_limit_bytes=VMEM_LIMIT
        ),
        cost_estimate=pl.CostEstimate(flops=9_000_000_000, bytes_accessed=20_000_000, transcendentals=0),
        name="reduce_all",
    )(normed, gate_back, up_back, gain_part.reshape(8, 128), tables)


def scatter_kernel(ids, grads, tables, rows, total, text_count, card, codes):
    frames = grads.shape[0]
    count = total.shape[0]

    def clear(i, carry):
        total[pl.ds(pl.multiple_of(i * 256, 256), 256)] = jnp.zeros((256, 128), F32)
        return carry

    lax.fori_loop(0, count // 256, clear, 0)

    def widen(i, carry):
        block = grads[pl.ds(i * 16, 16)].astype(F32).reshape(128, 128)
        rows[pl.ds(pl.multiple_of(i * 128, 128), 128)] = block
        return carry

    lax.fori_loop(0, frames // 16, widen, 0)

    def body(f, carry):
        places = [ids[k * frames + f] for k in range(codes + 1)]
        sums = [
            total[pl.ds(places[k], 1)] + rows[pl.ds(f * (codes + 1) + k, 1)]
            for k in range(codes + 1)
        ]
        for k in range(codes + 1):
            total[pl.ds(places[k], 1)] = sums[k]
        return carry

    lax.fori_loop(0, frames, body, 0, unroll=4)

    text_block, code_block = text_count // 16, card // 16
    for block in range(16):
        z_hi, y, core = block // 8, block // 2 % 4, block % 2
        tables[core, y, z_hi, :text_block] = total[
            block * text_block : (block + 1) * text_block
        ].astype(BF16)
        for c in range(codes):
            first = text_count + c * card + block * code_block
            tables[core, y, z_hi, pl.ds(text_block + c * code_block, code_block)] = total[
                first : first + code_block
            ].astype(BF16)


def scatter_rows(ids, grads, text_count, card, codes):
    rows = text_count // 16 + codes * card // 16
    return pl.pallas_call(
        functools.partial(scatter_kernel, text_count=text_count, card=card, codes=codes),
        out_shape=jax.ShapeDtypeStruct((2, 4, 2, rows, 128), BF16),
        in_specs=[pl.BlockSpec(memory_space=pltpu.SMEM), pl.BlockSpec(memory_space=pltpu.VMEM)],
        out_specs=pl.BlockSpec(memory_space=pltpu.VMEM),
        scratch_shapes=[
            pltpu.VMEM((grads.shape[0] * (codes + 1), 128), F32),
            pltpu.VMEM((text_count + codes * card, 128), F32),
        ],
        compiler_params=pltpu.CompilerParams(vmem_limit_bytes=VMEM_LIMIT),
        name="scatter_rows",
    )(ids, grads)


def on_device(
    temporal_out,
    context_weight,
    text_ids,
    code_ids,
    text_table,
    code_tables,
    norm_gain,
    gate_weight,
    up_weight,
    hidden_grad,
    stream_grad,
):
    code_count = code_tables.shape[0]
    card_size = code_tables.shape[1]
    own_frames = hidden_grad.shape[0]
    step_count = hidden_grad.shape[1]
    model_width = gate_weight.shape[0]
    hidden_width = gate_weight.shape[1]
    code_offsets = jnp.arange(code_count, dtype=jnp.int32)[None, :] * card_size
    text_rows = jnp.take(text_table, text_ids, axis=0)
    code_rows = jnp.take(
        code_tables.reshape(code_count * card_size, -1), code_ids + code_offsets, axis=0
    )
    embedded = jnp.concatenate([text_rows[:, None, :], code_rows], axis=1)
    partial_value = jnp.dot(temporal_out, context_weight, preferred_element_type=jnp.float32)
    context_slice = lax.psum_scatter(
        partial_value.astype(jnp.bfloat16), "tp", scatter_dimension=1, tiled=True
    ).astype(jnp.float32)
    feature_rows = (context_slice[:, None, :] + embedded.astype(jnp.float32)).astype(jnp.bfloat16)
    depth_in = lax.all_to_all(feature_rows, "tp", split_axis=0, concat_axis=2, tiled=True)
    depth_rows = depth_in.reshape(-1, model_width).astype(jnp.float32)
    inv_rms = lax.rsqrt(jnp.mean(depth_rows * depth_rows, axis=1, keepdims=True) + EPSILON)
    unit_rows = depth_rows * inv_rms
    normed = (unit_rows * norm_gain).astype(jnp.bfloat16)
    gate_values = jnp.dot(normed, gate_weight, preferred_element_type=jnp.float32)
    up_values = jnp.dot(normed, up_weight, preferred_element_type=jnp.float32)
    gate_sigmoid = jax.nn.sigmoid(gate_values)
    upstream = hidden_grad.reshape(-1, hidden_width).astype(jnp.float32)
    gate_back = (
        upstream * up_values * gate_sigmoid * (1.0 + gate_values * (1.0 - gate_sigmoid))
    ).astype(jnp.bfloat16)
    up_back = (upstream * gate_values * gate_sigmoid).astype(jnp.bfloat16)
    transposed = (((1,), (1,)), ((), ()))
    normed_back = lax.dot_general(
        gate_back, gate_weight, transposed, preferred_element_type=jnp.float32
    )
    normed_back = normed_back + lax.dot_general(
        up_back, up_weight, transposed, preferred_element_type=jnp.float32
    )
    gain_part = jnp.sum(normed_back * unit_rows, axis=0)
    scaled_back = normed_back * norm_gain
    stream_rows = stream_grad.reshape(-1, model_width).astype(jnp.float32)
    depth_back = stream_rows + inv_rms * (
        scaled_back - unit_rows * jnp.mean(scaled_back * unit_rows, axis=1, keepdims=True)
    )
    depth_grid = depth_back.astype(jnp.bfloat16).reshape(own_frames, step_count, model_width)
    context_grad = jnp.sum(depth_grid.astype(jnp.float32), axis=1).astype(jnp.bfloat16)
    feature_grid = lax.all_to_all(depth_grid, "tp", split_axis=2, concat_axis=0, tiled=True)
    places = jnp.concatenate(
        [text_ids[None], code_ids.T + code_offsets.T + text_table.shape[0]], axis=0
    ).reshape(-1)
    tables = scatter_rows(places, feature_grid, text_table.shape[0], card_size, code_count)
    gate_grad, up_grad, gain_sum, text_grad, code_sum = reduce_all(
        normed, gate_back, up_back, gain_part, tables
    )
    own_place = lax.axis_index("seq") * lax.axis_size("tp") + lax.axis_index("tp")
    gain_grad = lax.dynamic_slice_in_dim(gain_sum.reshape(-1), own_place * 8, 8)
    code_grad = code_sum.reshape(code_count, -1, code_sum.shape[1])
    return (gate_grad, up_grad, gain_grad, text_grad, code_grad, context_grad)


def solution(mesh):
    return jax.shard_map(
        on_device,
        mesh=mesh,
        in_specs=(
            P("seq", "tp"),
            P("tp", None),
            P("seq"),
            P("seq", None),
            P(None, "tp"),
            P(None, None, "tp"),
            P(),
            P(),
            P(),
            P(("seq", "tp"), None, None),
            P(("seq", "tp"), None, None),
        ),
        out_specs=(
            P(("seq", "tp"), None),
            P(("seq", "tp"), None),
            P(("seq", "tp")),
            P("seq", "tp"),
            P(None, "seq", "tp"),
            P(("seq", "tp"), None),
        ),
        check_vma=False,
    )
```

```python
import functools

import jax
import jax.numpy as jnp
from jax import lax
from jax.experimental import pallas as pl
from jax.experimental.pallas import tpu as pltpu
from jax.sharding import PartitionSpec as P

EPSILON = 1e-05

MESH = pl.DeviceIdType.MESH
F32 = jnp.float32
BF16 = jnp.bfloat16
VMEM_LIMIT = 60 * 1024 * 1024


def position():
    seq = lax.axis_index("seq")
    tp = lax.axis_index("tp")
    core = lax.rem(seq, 2)
    y = lax.rem(lax.div(seq, 2), 4)
    z_hi = lax.div(seq, 8)
    x = lax.div(tp, 2)
    z_lo = lax.rem(tp, 2)
    return core, x, y, z_hi * 2 + z_lo


def device_at(core, x, y, z):
    seq = (lax.div(z, 2) * 4 + y) * 2 + core
    tp = x * 2 + lax.rem(z, 2)
    return (seq, tp)


def step_to(value, by):
    return lax.rem(value + by, 4)


def greet(devices):
    barrier = pltpu.get_barrier_semaphore()
    for device in devices:
        pl.semaphore_signal(barrier, inc=1, device_id=device, device_id_type=MESH)
    pl.semaphore_wait(barrier, len(devices))


class Copies:
    def __init__(self, send_sems, recv_sems):
        self.send_sems, self.recv_sems, self.made = send_sems, recv_sems, []

    def send(self, source, target, device):
        at = len(self.made)
        copy = pltpu.make_async_remote_copy(
            src_ref=source,
            dst_ref=target,
            send_sem=self.send_sems.at[at],
            recv_sem=self.recv_sems.at[at],
            device_id=device,
            device_id_type=MESH,
        )
        copy.start()
        self.made.append(copy)
        return copy

    def finish(self):
        for copy in self.made:
            copy.wait_send()


class Ring:
    def __init__(self, copies, here, device, part, pass_on, direct, ended):
        self.copies, self.here, self.device, self.part = copies, here, device, part
        self.pass_on, self.direct, self.ended = pass_on, direct, ended

    def first(self):
        up, down, far = (step_to(self.here, by) for by in (1, 3, 2))
        up_device, down_device = self.device(up), self.device(down)
        send = self.copies.send
        self.from_down = send(self.part(far, 0), self.pass_on(0), up_device)
        self.from_up = send(self.part(far, 1), self.pass_on(1), down_device)
        self.near = [
            send(self.part(up, 1), self.direct(1), up_device),
            send(self.part(down, 0), self.direct(0), down_device),
        ]

    def second(self, add):
        up, down = step_to(self.here, 1), step_to(self.here, 3)
        self.from_down.wait_recv()
        add(self.part(up, 0), [self.part(up, 0), self.pass_on(0)])
        last_up = self.copies.send(self.part(up, 0), self.ended(0), self.device(up))
        self.from_up.wait_recv()
        add(self.part(down, 1), [self.part(down, 1), self.pass_on(1)])
        last_down = self.copies.send(self.part(down, 1), self.ended(1), self.device(down))
        self.last = [last_up, last_down]

    def third(self, add, out):
        for copy in self.near + self.last:
            copy.wait_recv()
        for half in (0, 1):
            add(out(half), [self.part(self.here, half), self.direct(half), self.ended(half)])


class Exchange:
    def __init__(self, copies, x, z_lo, device, chunk, landing, relay):
        self.copies, self.x, self.z_lo, self.device = copies, x, z_lo, device
        self.chunk, self.landing, self.relay = chunk, landing, relay
        self.relays, self.arrivals = [], []

    def place(self, by_x, by_z):
        z_lo = self.z_lo if by_z == 0 else 1 - self.z_lo
        return step_to(self.x, by_x) * 2 + z_lo

    def start(self, by_x, by_z):
        own, there = self.place(0, 0), self.place(by_x, by_z)
        send = self.copies.send
        if by_x == 2:
            for half, by in ((0, 1), (1, 3)):
                copy = send(self.chunk(there, half), self.relay(by_z, half), self.device(self.place(by, by_z)))
                self.relays.append((copy, by_z, half))
        else:
            self.arrivals.append(send(self.chunk(there, None), self.landing(own, None), self.device(there)))

    def forward(self):
        for copy, by_z, half in self.relays:
            copy.wait_recv()
            came, by = ((3, 1), (1, 3))[half]
            target = self.landing(self.place(came, by_z), half)
            self.arrivals.append(
                self.copies.send(self.relay(by_z, half), target, self.device(self.place(by, 0)))
            )

    def arrive(self):
        for copy in self.arrivals:
            copy.wait_recv()


ORDER = ((2, 1), (2, 0), (1, 1), (3, 1), (1, 0), (3, 0), (0, 1), (0, 0))
TILES = 4


def front_kernel(
    ids, text_table, code_tables, temporal, context_weight, gain, gate_weight, up_weight, hidden, stream,
    normed_out, gate_out, up_out, gain_out, context_out, grid_out,
    table, staged, table_sems, picked,
    c_term, c_pass, c_direct, c_ended, c_pair, c_last, context,
    e_send, e_in, e_relay, g_send, g_relay,
    gate_w, up_w, hidden_in, stream_in, load_sems,
    normed, gate_back, up_back, out_sems, unit, scale, back, context_grad, send_sems, recv_sems,
):
    core, x, y, z = position()
    z_lo = lax.rem(z, 2)
    own = x * 2 + z_lo
    frames_all = temporal.shape[0]
    frames = frames_all // 8
    tile = frames // TILES
    rows = tile * 8
    half_rows = rows // 2
    seq = lax.axis_index("seq")
    device = lambda place: (seq, place)
    copies = Copies(send_sems, recv_sems)

    loads = []
    for at, (source, target) in enumerate(
        ((gate_weight, gate_w), (up_weight, up_w), (hidden, hidden_in), (stream, stream_in))
    ):
        loads.append(pltpu.make_async_copy(source, target, load_sems.at[at]))

    block = staged.shape[1]
    text_blocks = text_table.shape[0] // block
    blocks = table.shape[0] // block

    def load_block(i):
        source = text_table if i < text_blocks else code_tables
        first = (i if i < text_blocks else i - text_blocks) * block
        return pltpu.make_async_copy(
            source.at[pl.ds(first, block)], staged.at[i % 2], table_sems.at[i % 2]
        )

    block_loads = [load_block(i) for i in range(blocks)]
    block_loads[0].start()
    block_loads[1].start()
    for load in loads:
        load.start()
    greet([device(lax.rem(own + by, 8)) for by in range(1, 8)])

    def context_body(i, carry):
        block_rows = pl.ds(pl.multiple_of(i * frames, frames), frames)
        partial = jnp.dot(temporal[block_rows], context_weight[...], preferred_element_type=F32)
        c_term[lax.div(i, 2), lax.rem(i, 2)] = partial.astype(BF16)
        return carry

    lax.fori_loop(0, 8, context_body, 0)
    half_width = c_term.shape[-1] // 2
    c_half = lambda half: pl.ds(half * half_width, half_width)
    c_pick = lambda ref: lambda half: ref.at[:, :, c_half(half)]
    c_ring = Ring(
        copies, x, lambda at: device(at * 2 + z_lo),
        lambda at, half: c_term.at[at, :, :, c_half(half)],
        c_pick(c_pass), c_pick(c_direct), c_pick(c_ended),
    )
    c_ring.first()

    def add_context(out, refs):
        def body(i, carry):
            at = pl.ds(pl.multiple_of(lax.rem(i, frames // 16) * 16, 16), 16)
            low = lax.div(i, frames // 16)
            total = refs[0][low, at].astype(F32)
            for ref in refs[1:]:
                total = total + ref[low, at].astype(F32)
            out[low, at] = total.astype(BF16)
            return carry

        lax.fori_loop(0, frames // 8, body, 0)

    for i in range(blocks):
        block_loads[i].wait()

        def widen(j, carry):
            at = pl.multiple_of(j * 128, 128)
            table[pl.ds(i * block + at, 128)] = staged[i % 2, pl.ds(at, 128)].astype(F32)
            return carry

        lax.fori_loop(0, block // 128, widen, 0)
        if i + 2 < blocks:
            block_loads[i + 2].start()

    def gather(t, place, target):
        def body(f, carry):
            frame = place * frames + t * tile + f
            for k in range(8):
                picked[pl.ds(f * 8 + k, 1)] = table[pl.ds(ids[k * frames_all + frame], 1)]
            return carry

        lax.fori_loop(0, tile, body, 0, unroll=4)
        target[...] = picked[...].astype(BF16)

    def tile_rows(t, half):
        if half is None:
            return pl.ds(t * rows, rows)
        return pl.ds(t * rows + half * half_rows, half_rows)

    def exchange(t, send_ref, in_ref, relay_ref):
        return Exchange(
            copies, x, z_lo, device,
            lambda place, half: send_ref.at[place, tile_rows(t, half)],
            lambda place, half: in_ref.at[place, tile_rows(t, half)],
            lambda by_z, half: relay_ref.at[t, by_z, half],
        )

    rows_in = [exchange(t, e_send, e_in, e_relay) for t in range(TILES)]
    rows_back = [exchange(t, g_send, grid_out, g_relay) for t in range(TILES)]

    def gather_tile(t):
        for by_x, by_z in ORDER:
            place = rows_in[t].place(by_x, by_z)
            if (by_x, by_z) == (0, 0):
                gather(t, place, e_in.at[place, tile_rows(t, None)])
            else:
                gather(t, place, e_send.at[place, tile_rows(t, None)])
                rows_in[t].start(by_x, by_z)

    gather_tile(0)
    c_ring.second(add_context)
    gather_tile(1)
    rows_in[0].forward()
    c_ring.third(add_context, lambda half: c_pair.at[:, :, c_half(half)])
    c_copy = copies.send(c_pair.at[1 - z_lo], c_last, device(x * 2 + 1 - z_lo))
    gather_tile(2)
    rows_in[1].forward()
    gather_tile(3)
    rows_in[2].forward()
    c_copy.wait_recv()

    def context_total(i, carry):
        at = pl.ds(pl.multiple_of(i * 16, 16), 16)
        context[at] = c_pair[z_lo, at].astype(F32) + c_last[at].astype(F32)
        return carry

    lax.fori_loop(0, frames // 16, context_total, 0)

    width = context.shape[1]
    column_blocks = width // 128
    gain_out[...] = jnp.zeros(gain_out.shape, F32)
    for load in loads:
        load.wait()

    def run_tile(t):
        slot = t % 2
        rows_in[t].arrive()

        def norm(i, carry):
            first = t * rows + i * 32
            at = pl.ds(pl.multiple_of(i * 32, 32), 32)
            frame_rows = [
                context[pl.ds(t * tile + i * 4 + f, 1)] for f in range(4)
            ]
            spread = jnp.concatenate([jnp.broadcast_to(row, (8, width)) for row in frame_rows], axis=0)
            embedded = jnp.concatenate(
                [e_in[j, pl.ds(pl.multiple_of(first, 32), 32)] for j in range(column_blocks)], axis=1
            )
            depth = (spread + embedded.astype(F32)).astype(BF16).astype(F32)
            inv = lax.rsqrt(jnp.mean(depth * depth, axis=1, keepdims=True) + EPSILON)
            unit_rows = depth * inv
            unit[at] = unit_rows
            scale[at] = jnp.broadcast_to(inv, (32, 128))
            normed[slot, at] = (unit_rows * gain[...]).astype(BF16)
            return carry

        lax.fori_loop(0, rows // 32, norm, 0)

        def forward_pass(j, carry):
            columns = pl.ds(pl.multiple_of(j * 256, 256), 256)
            left = normed[slot]
            gate = jnp.dot(left, gate_w[:, columns], preferred_element_type=F32)
            up = jnp.dot(left, up_w[:, columns], preferred_element_type=F32)
            upstream = hidden_in[pl.ds(t * rows, rows), columns].astype(F32)
            sigma = jax.nn.sigmoid(gate)
            with_sigma = upstream * sigma
            gate_back[slot, :, columns] = (with_sigma * up * (1.0 + gate * (1.0 - sigma))).astype(BF16)
            up_back[slot, :, columns] = (with_sigma * gate).astype(BF16)
            return carry

        lax.fori_loop(0, gate_w.shape[1] // 256, forward_pass, 0)
        outs = [
            pltpu.make_async_copy(ref.at[slot], target.at[pl.ds(t * rows, rows)], out_sems.at[slot, n])
            for n, (ref, target) in enumerate(
                ((normed, normed_out), (gate_back, gate_out), (up_back, up_out))
            )
        ]
        for out in outs:
            out.start()

        transposed = (((1,), (1,)), ((), ()))

        def backward_pass(j, carry):
            columns = pl.ds(pl.multiple_of(j * 256, 256), 256)
            total = lax.dot_general(
                gate_back[slot], gate_w[columns], transposed, preferred_element_type=F32
            )
            total = total + lax.dot_general(
                up_back[slot], up_w[columns], transposed, preferred_element_type=F32
            )
            back[:, columns] = total
            return carry

        lax.fori_loop(0, width // 256, backward_pass, 0)

        def finish(i, carry):
            at = pl.ds(pl.multiple_of(i * 64, 64), 64)
            whole = pl.ds(pl.multiple_of(t * rows + i * 64, 64), 64)
            normed_back, unit_rows = back[at], unit[at]
            gain_out[...] += jnp.sum((normed_back * unit_rows).reshape(8, 8, width), axis=0)
            scaled = normed_back * gain[...]
            mean = jnp.mean(scaled * unit_rows, axis=1, keepdims=True)
            depth = stream_in[whole].astype(F32) + scale[at, :1] * (scaled - unit_rows * mean)
            depth = depth.astype(BF16)
            for j in range(column_blocks):
                g_send[j, whole] = depth[:, j * 128 : (j + 1) * 128]
            frame_rows = pl.ds(pl.multiple_of(t * tile + i * 8, 8), 8)
            context_grad[frame_rows] = jnp.sum(depth.astype(F32).reshape(8, 8, width), axis=1)
            return carry

        lax.fori_loop(0, rows // 64, finish, 0)
        for by_x, by_z in ORDER[:-1]:
            rows_back[t].start(by_x, by_z)
        grid_out[own, pl.ds(t * rows, rows)] = g_send[own, pl.ds(t * rows, rows)]
        return outs

    outs = [run_tile(0)]
    rows_in[3].forward()
    outs.append(run_tile(1))
    rows_back[0].forward()
    for out in outs[0]:
        out.wait()
    outs.append(run_tile(2))
    rows_back[1].forward()
    for out in outs[1]:
        out.wait()
    outs.append(run_tile(3))
    rows_back[2].forward()
    context_out[...] = context_grad[...].astype(BF16)
    rows_back[3].forward()
    for out in outs[2] + outs[3]:
        out.wait()
    for t in range(TILES):
        rows_back[t].arrive()
    copies.finish()


def front(ids, text_table, code_tables, temporal, context_weight, gain, gate_weight, up_weight, hidden, stream):
    frames_all = temporal.shape[0]
    frames = frames_all // 8
    width, hidden_width = gate_weight.shape
    rows = frames * 8 // TILES
    bf = lambda *shape: pltpu.VMEM(shape, BF16)
    f32 = lambda *shape: pltpu.VMEM(shape, F32)
    dma = lambda *shape: pltpu.SemaphoreType.DMA(shape)
    vmem = pl.BlockSpec(memory_space=pltpu.VMEM)
    anywhere = pl.BlockSpec(memory_space=pl.ANY)
    table_rows = text_table.shape[0] + code_tables.shape[0]
    return pl.pallas_call(
        front_kernel,
        out_shape=(
            jax.ShapeDtypeStruct((frames * 8, width), BF16),
            jax.ShapeDtypeStruct((frames * 8, hidden_width), BF16),
            jax.ShapeDtypeStruct((frames * 8, hidden_width), BF16),
            jax.ShapeDtypeStruct((8, width), F32),
            jax.ShapeDtypeStruct((frames, width), BF16),
            jax.ShapeDtypeStruct((8, frames * 8, 128), BF16),
        ),
        in_specs=[pl.BlockSpec(memory_space=pltpu.SMEM), anywhere, anywhere, vmem, vmem, vmem]
        + [anywhere] * 4,
        out_specs=(anywhere, anywhere, anywhere, vmem, vmem, vmem),
        scratch_shapes=[
            f32(table_rows, 128), bf(2, 2048, 128), dma(2), f32(rows, 128),
            bf(4, 2, frames, width), bf(2, frames, width), bf(2, frames, width), bf(2, frames, width),
            bf(2, frames, width), bf(frames, width), f32(frames, width),
            bf(8, frames * 8, 128), bf(8, frames * 8, 128), bf(TILES, 2, 2, rows // 2, 128),
            bf(8, frames * 8, 128), bf(TILES, 2, 2, rows // 2, 128),
            bf(width, hidden_width), bf(width, hidden_width),
            bf(frames * 8, hidden_width), bf(frames * 8, width), dma(4),
            bf(2, rows, width), bf(2, rows, hidden_width), bf(2, rows, hidden_width), dma(2, 3),
            f32(rows, width), f32(rows, 128), f32(rows, width), f32(frames, width),
            dma(120), dma(120),
        ],
        compiler_params=pltpu.CompilerParams(
            collective_id=2, has_side_effects=True, vmem_limit_bytes=VMEM_LIMIT
        ),
        cost_estimate=pl.CostEstimate(
            flops=19_000_000_000, bytes_accessed=40_000_000, transcendentals=2_000_000
        ),
        name="front",
    )(ids, text_table, code_tables, temporal, context_weight, gain, gate_weight, up_weight, hidden, stream)


def reduce_kernel(
    normed, gate_back, up_back, gain, tables,
    gate_out, up_out, gain_out, text_out, code_out,
    turned, term, pair, x_pass, x_direct, x_ended, z_term, z_pass, z_direct, z_ended,
    y_term, y_pass, y_direct, y_ended, own, other, t_pass, t_direct, t_ended, t_sum, t_last,
    gain_own, gain_in, local_sem, send_sems, recv_sems,
):
    core, x, y, z = position()
    half_width = term.shape[-1] // 2
    text_rows = text_out.shape[0]
    table_rows = own.shape[2]
    half_rows = table_rows // 2
    z_hi = lax.div(z, 2)
    sibling = device_at(1 - core, x, y, z)
    x_device = lambda at: device_at(core, at, y, z)
    y_device = lambda at: device_at(core, x, at, z)
    z_device = lambda at: device_at(core, x, y, at)
    greet(
        [sibling]
        + [x_device(step_to(x, by)) for by in (1, 2, 3)]
        + [y_device(step_to(y, by)) for by in (1, 2, 3)]
        + [z_device(step_to(z, by)) for by in (1, 2, 3)]
    )
    copies = Copies(send_sems, recv_sems)
    halves = lambda half: pl.ds(half * half_width, half_width)

    keep = pltpu.make_async_copy(tables.at[core], own, local_sem)
    keep.start()
    table_pairs = [
        copies.send(tables.at[1 - core, i], other.at[i], sibling) for i in range(4)
    ]
    gain_own[0] = gain[...]
    gain_copy = copies.send(gain_own.at[0], gain_in.at[0], sibling)

    def make_term(q):
        turned[...] = normed[:, q * 256 : (q + 1) * 256].T

        def body(i, carry):
            columns = pl.ds(pl.multiple_of(i * 256, 256), 256)
            left = turned[...]
            gate = jnp.dot(left, gate_back[:, columns], preferred_element_type=F32)
            up = jnp.dot(left, up_back[:, columns], preferred_element_type=F32)
            both = jnp.concatenate([gate.reshape(32, 8, 256), up.reshape(32, 8, 256)], axis=1)
            both = both.astype(BF16).reshape(2, 2, 4, 2, 16, 256)
            for low in range(2):
                term[:, :, q * 2 + low, :, :, columns] = both[low]
            return carry

        lax.fori_loop(0, gate_back.shape[1] // 256, body, 0)

    pair_copies = []

    def send_pair(q):
        rows = pl.ds(q * 2, 2)
        pair_copies.append(copies.send(term.at[1 - core, :, rows], pair.at[:, rows], sibling))

    def add_pair(q):
        pair_copies[q].wait_recv()

        def body(i, carry):
            column, rest = lax.div(i, 4), lax.rem(i, 4)
            row, low = q * 2 + lax.div(rest, 2), lax.rem(rest, 2)
            here = term[core, column, row, low].astype(F32)
            term[core, column, row, low] = (here + pair[column, row, low].astype(F32)).astype(BF16)
            return carry

        lax.fori_loop(0, 16, body, 0)

    def add_four(out, refs):
        def body(i, carry):
            row, low = lax.div(i, 2), lax.rem(i, 2)
            total = refs[0][row, low].astype(F32)
            for ref in refs[1:]:
                total = total + ref[row, low].astype(F32)
            out[row, low] = total.astype(BF16)
            return carry

        lax.fori_loop(0, 4, body, 0)

    def x_ring(q):
        rows = pl.ds(q * 2, 2)
        pick = lambda ref: lambda half: ref.at[rows, :, :, halves(half)]
        return Ring(
            copies, x, x_device,
            lambda at, half: term.at[core, at, rows, :, :, halves(half)],
            pick(x_pass), pick(x_direct), pick(x_ended),
        )

    x_rings = [x_ring(q) for q in range(4)]

    def x_out(q):
        def finish(out, refs):
            def body(i, carry):
                row, low = lax.div(i, 2), lax.rem(i, 2)
                total = refs[0][row, low].astype(F32)
                for ref in refs[1:]:
                    total = total + ref[row, low].astype(F32)
                z_term[q // 2 * 2 + low, q % 2 * 2 + row, :, out] = total.astype(BF16)
                return carry

            lax.fori_loop(0, 4, body, 0)

        x_rings[q].third(finish, halves)

    t_half = lambda half: pl.ds(half * half_rows, half_rows)
    t_pick = lambda ref: lambda half: ref.at[:, t_half(half)]
    t_ring = Ring(
        copies, y, y_device,
        lambda at, half: own.at[at, :, t_half(half)],
        t_pick(t_pass), t_pick(t_direct), t_pick(t_ended),
    )

    def add_tables(out, refs):
        def body(i, carry):
            rows = pl.ds(pl.multiple_of(i * 64, 64), 64)
            for hi in range(2):
                total = refs[0][hi, rows].astype(F32)
                for ref in refs[1:]:
                    total = total + ref[hi, rows].astype(F32)
                out[hi, rows] = total.astype(BF16)
            return carry

        lax.fori_loop(0, half_rows // 64, body, 0)

    def pair_tables():
        keep.wait()
        for copy in table_pairs:
            copy.wait_recv()

        def body(i, carry):
            rows = pl.ds(pl.multiple_of(lax.rem(i, table_rows // 64) * 64, 64), 64)
            at = lax.div(i, table_rows // 64)
            for hi in range(2):
                total = own[at, hi, rows].astype(F32) + other[at, hi, rows].astype(F32)
                own[at, hi, rows] = total.astype(BF16)
            return carry

        lax.fori_loop(0, 4 * table_rows // 64, body, 0)

    def gain_round(index, device, here):
        gain_own[index] = gain_own[index - 1] + gain_sum
        return [
            copies.send(gain_own.at[index], gain_in.at[index * 3 + by - 3], device(step_to(here, by)))
            for by in (1, 2, 3)
        ]

    def gain_total(waited, slots):
        for copy in waited:
            copy.wait_recv()
        total = gain_in[slots[0]]
        for slot in slots[1:]:
            total = total + gain_in[slot]
        return total

    make_term(0)
    send_pair(0)
    pair_tables()
    t_ring.first()
    make_term(1)
    send_pair(1)
    add_pair(0)
    x_rings[0].first()
    gain_sum = gain_total([gain_copy], [0])
    gain_copies = gain_round(1, x_device, x)
    make_term(2)
    send_pair(2)
    add_pair(1)
    x_rings[1].first()
    t_ring.second(add_tables)
    make_term(3)
    send_pair(3)
    add_pair(2)
    x_rings[2].first()
    x_rings[0].second(add_four)
    add_pair(3)
    x_rings[3].first()
    x_rings[1].second(add_four)
    gain_sum = gain_total(gain_copies, [1, 2, 3])
    gain_copies = gain_round(2, y_device, y)
    x_out(0)
    x_rings[2].second(add_four)
    x_out(1)
    t_ring.third(add_tables, lambda half: t_sum.at[:, t_half(half)])
    t_copy = copies.send(t_sum.at[1 - z_hi], t_last, z_device(step_to(z, 2)))
    x_rings[3].second(add_four)
    x_out(2)
    gain_sum = gain_total(gain_copies, [4, 5, 6])
    gain_copies = gain_round(3, z_device, z)
    x_out(3)

    def add_few(out, refs):
        for i in range(4):
            total = refs[0][i].astype(F32)
            for ref in refs[1:]:
                total = total + ref[i].astype(F32)
            out[i] = total.astype(BF16)

    z_pick = lambda ref: lambda half: ref.at[:, :, halves(half)]
    z_ring = Ring(
        copies, z, z_device,
        lambda at, half: z_term.at[at, :, :, halves(half)],
        z_pick(z_pass), z_pick(z_direct), z_pick(z_ended),
    )
    z_ring.first()
    z_ring.second(add_few)
    z_ring.third(add_few, lambda half: y_term.at[:, :, halves(half)])

    def add_one(out, refs):
        total = refs[0][...].astype(F32)
        for ref in refs[1:]:
            total = total + ref[...].astype(F32)
        out[...] = total.astype(BF16)

    y_pick = lambda ref: lambda half: ref.at[:, halves(half)]
    y_ring = Ring(
        copies, y, y_device,
        lambda at, half: y_term.at[at, :, halves(half)],
        y_pick(y_pass), y_pick(y_direct), y_pick(y_ended),
    )
    y_ring.first()
    t_copy.wait_recv()

    def text_body(i, carry):
        rows = pl.ds(pl.multiple_of(i * 64, 64), 64)
        text_out[rows] = t_sum[z_hi, rows].astype(F32) + t_last[rows].astype(F32)
        return carry

    lax.fori_loop(0, text_rows // 64, text_body, 0)

    def code_body(i, carry):
        at = pl.ds(pl.multiple_of(i * 64, 64), 64)
        rows = pl.ds(pl.multiple_of(text_rows + i * 64, 64), 64)
        code_out[at] = t_sum[z_hi, rows].astype(F32) + t_last[rows].astype(F32)
        return carry

    lax.fori_loop(0, code_out.shape[0] // 64, code_body, 0)
    gain_out[...] = gain_own[3] + gain_total(gain_copies, [7, 8, 9])
    y_ring.second(add_one)

    def finish_weights(out, refs):
        total = refs[0][...].astype(F32)
        for ref in refs[1:]:
            total = total + ref[...].astype(F32)
        gate_out[:, out] = total[:8]
        up_out[:, out] = total[8:]

    y_ring.third(finish_weights, halves)
    copies.finish()


def reduce_all(normed, gate_back, up_back, gain_part, tables):
    features, width = normed.shape[1], gate_back.shape[1]
    table_rows = tables.shape[3]
    text_rows = table_rows * 8 // 15
    out_rows = features // 128
    bf = lambda *shape: pltpu.VMEM(shape, BF16)
    vmem = pl.BlockSpec(memory_space=pltpu.VMEM)
    return pl.pallas_call(
        reduce_kernel,
        out_shape=(
            jax.ShapeDtypeStruct((out_rows, width), F32),
            jax.ShapeDtypeStruct((out_rows, width), F32),
            jax.ShapeDtypeStruct((8, 128), F32),
            jax.ShapeDtypeStruct((text_rows, 128), F32),
            jax.ShapeDtypeStruct((table_rows - text_rows, 128), F32),
        ),
        in_specs=[vmem] * 4 + [pl.BlockSpec(memory_space=pl.ANY)],
        out_specs=(vmem,) * 5,
        scratch_shapes=[
            bf(256, normed.shape[0]),
            bf(2, 4, 8, 2, 16, width),
            bf(4, 8, 2, 16, width),
            bf(8, 2, 16, width), bf(8, 2, 16, width), bf(8, 2, 16, width),
            bf(4, 4, 16, width), bf(4, 16, width), bf(4, 16, width), bf(4, 16, width),
            bf(4, 16, width), bf(16, width), bf(16, width), bf(16, width),
            bf(4, 2, table_rows, 128), bf(4, 2, table_rows, 128),
            bf(2, table_rows, 128), bf(2, table_rows, 128), bf(2, table_rows, 128),
            bf(2, table_rows, 128), bf(table_rows, 128),
            pltpu.VMEM((4, 8, 128), F32), pltpu.VMEM((10, 8, 128), F32),
            pltpu.SemaphoreType.DMA,
            pltpu.SemaphoreType.DMA((64,)),
            pltpu.SemaphoreType.DMA((64,)),
        ],
        compiler_params=pltpu.CompilerParams(
            collective_id=1, has_side_effects=True, vmem_limit_bytes=VMEM_LIMIT
        ),
        cost_estimate=pl.CostEstimate(flops=9_000_000_000, bytes_accessed=20_000_000, transcendentals=0),
        name="reduce_all",
    )(normed, gate_back, up_back, gain_part.reshape(8, 128), tables)


def scatter_kernel(ids, grads, tables, rows, total, text_count, card, codes):
    frames = grads.shape[0]
    count = total.shape[0]

    def clear(i, carry):
        total[pl.ds(pl.multiple_of(i * 256, 256), 256)] = jnp.zeros((256, 128), F32)
        return carry

    lax.fori_loop(0, count // 256, clear, 0)

    def widen(i, carry):
        block = grads[pl.ds(i * 16, 16)].astype(F32).reshape(128, 128)
        rows[pl.ds(pl.multiple_of(i * 128, 128), 128)] = block
        return carry

    lax.fori_loop(0, frames // 16, widen, 0)

    def body(f, carry):
        places = [ids[k * frames + f] for k in range(codes + 1)]
        sums = [
            total[pl.ds(places[k], 1)] + rows[pl.ds(f * (codes + 1) + k, 1)]
            for k in range(codes + 1)
        ]
        for k in range(codes + 1):
            total[pl.ds(places[k], 1)] = sums[k]
        return carry

    lax.fori_loop(0, frames, body, 0, unroll=4)

    text_block, code_block = text_count // 16, card // 16
    for block in range(16):
        z_hi, y, core = block // 8, block // 2 % 4, block % 2
        tables[core, y, z_hi, :text_block] = total[
            block * text_block : (block + 1) * text_block
        ].astype(BF16)
        for c in range(codes):
            first = text_count + c * card + block * code_block
            tables[core, y, z_hi, pl.ds(text_block + c * code_block, code_block)] = total[
                first : first + code_block
            ].astype(BF16)


def scatter_rows(ids, grads, text_count, card, codes):
    rows = text_count // 16 + codes * card // 16
    return pl.pallas_call(
        functools.partial(scatter_kernel, text_count=text_count, card=card, codes=codes),
        out_shape=jax.ShapeDtypeStruct((2, 4, 2, rows, 128), BF16),
        in_specs=[pl.BlockSpec(memory_space=pltpu.SMEM), pl.BlockSpec(memory_space=pltpu.VMEM)],
        out_specs=pl.BlockSpec(memory_space=pltpu.VMEM),
        scratch_shapes=[
            pltpu.VMEM((grads.shape[0] * (codes + 1), 128), F32),
            pltpu.VMEM((text_count + codes * card, 128), F32),
        ],
        compiler_params=pltpu.CompilerParams(vmem_limit_bytes=VMEM_LIMIT),
        name="scatter_rows",
    )(ids, grads)


def on_device(
    temporal_out,
    context_weight,
    text_ids,
    code_ids,
    text_table,
    code_tables,
    norm_gain,
    gate_weight,
    up_weight,
    hidden_grad,
    stream_grad,
):
    code_count, card_size, feature_width = code_tables.shape
    text_count = text_table.shape[0]
    code_offsets = jnp.arange(code_count, dtype=jnp.int32)[:, None] * card_size + text_count
    places = jnp.concatenate([text_ids[None], code_ids.T + code_offsets], axis=0).reshape(-1)
    normed, gate_back, up_back, gain_part, context_grad, grid = front(
        places,
        text_table,
        code_tables.reshape(code_count * card_size, feature_width),
        temporal_out,
        context_weight,
        norm_gain.reshape(1, -1),
        gate_weight,
        up_weight,
        hidden_grad.reshape(-1, hidden_grad.shape[2]),
        stream_grad.reshape(-1, stream_grad.shape[2]),
    )
    gain_part = jnp.sum(gain_part, axis=0)
    tables = scatter_rows(places, grid.reshape(-1, 8, feature_width), text_count, card_size, code_count)
    gate_grad, up_grad, gain_sum, text_grad, code_sum = reduce_all(
        normed, gate_back, up_back, gain_part, tables
    )
    own_place = lax.axis_index("seq") * lax.axis_size("tp") + lax.axis_index("tp")
    gain_grad = lax.dynamic_slice_in_dim(gain_sum.reshape(-1), own_place * 8, 8)
    code_grad = code_sum.reshape(code_count, -1, code_sum.shape[1])
    return (gate_grad, up_grad, gain_grad, text_grad, code_grad, context_grad)


def solution(mesh):
    return jax.shard_map(
        on_device,
        mesh=mesh,
        in_specs=(
            P("seq", "tp"),
            P("tp", None),
            P("seq"),
            P("seq", None),
            P(None, "tp"),
            P(None, None, "tp"),
            P(),
            P(),
            P(),
            P(("seq", "tp"), None, None),
            P(("seq", "tp"), None, None),
        ),
        out_specs=(
            P(("seq", "tp"), None),
            P(("seq", "tp"), None),
            P(("seq", "tp")),
            P("seq", "tp"),
            P(None, "seq", "tp"),
            P(("seq", "tp"), None),
        ),
        check_vma=False,
    )
```

```python
import functools

import jax
import jax.numpy as jnp
from jax import lax
from jax.experimental import pallas as pl
from jax.experimental.pallas import tpu as pltpu
from jax.sharding import PartitionSpec as P

EPSILON = 1e-05

MESH = pl.DeviceIdType.MESH
F32 = jnp.float32
BF16 = jnp.bfloat16
VMEM_LIMIT = 60 * 1024 * 1024


def position():
    seq = lax.axis_index("seq")
    tp = lax.axis_index("tp")
    core = lax.rem(seq, 2)
    y = lax.rem(lax.div(seq, 2), 4)
    z_hi = lax.div(seq, 8)
    x = lax.div(tp, 2)
    z_lo = lax.rem(tp, 2)
    return core, x, y, z_hi * 2 + z_lo


def device_at(core, x, y, z):
    seq = (lax.div(z, 2) * 4 + y) * 2 + core
    tp = x * 2 + lax.rem(z, 2)
    return (seq, tp)


def step_to(value, by):
    return lax.rem(value + by, 4)


def greet(devices):
    barrier = pltpu.get_barrier_semaphore()
    for device in devices:
        pl.semaphore_signal(barrier, inc=1, device_id=device, device_id_type=MESH)
    pl.semaphore_wait(barrier, len(devices))


class Copies:
    def __init__(self, send_sems, recv_sems):
        self.send_sems, self.recv_sems, self.made = send_sems, recv_sems, []

    def send(self, source, target, device):
        at = len(self.made)
        copy = pltpu.make_async_remote_copy(
            src_ref=source,
            dst_ref=target,
            send_sem=self.send_sems.at[at],
            recv_sem=self.recv_sems.at[at],
            device_id=device,
            device_id_type=MESH,
        )
        copy.start()
        self.made.append(copy)
        return copy

    def finish(self):
        for copy in self.made:
            copy.wait_send()


class Ring:
    def __init__(self, copies, here, device, part, pass_on, direct, ended):
        self.copies, self.here, self.device, self.part = copies, here, device, part
        self.pass_on, self.direct, self.ended = pass_on, direct, ended

    def first(self):
        up, down, far = (step_to(self.here, by) for by in (1, 3, 2))
        up_device, down_device = self.device(up), self.device(down)
        send = self.copies.send
        self.from_down = send(self.part(far, 0), self.pass_on(0), up_device)
        self.from_up = send(self.part(far, 1), self.pass_on(1), down_device)
        self.near = [
            send(self.part(up, 1), self.direct(1), up_device),
            send(self.part(down, 0), self.direct(0), down_device),
        ]

    def second(self, add):
        up, down = step_to(self.here, 1), step_to(self.here, 3)
        self.from_down.wait_recv()
        add(self.part(up, 0), [self.part(up, 0), self.pass_on(0)])
        last_up = self.copies.send(self.part(up, 0), self.ended(0), self.device(up))
        self.from_up.wait_recv()
        add(self.part(down, 1), [self.part(down, 1), self.pass_on(1)])
        last_down = self.copies.send(self.part(down, 1), self.ended(1), self.device(down))
        self.last = [last_up, last_down]

    def third(self, add, out):
        for copy in self.near + self.last:
            copy.wait_recv()
        for half in (0, 1):
            add(out(half), [self.part(self.here, half), self.direct(half), self.ended(half)])


class Exchange:
    def __init__(self, copies, x, z_lo, device, chunk, landing, relay):
        self.copies, self.x, self.z_lo, self.device = copies, x, z_lo, device
        self.chunk, self.landing, self.relay = chunk, landing, relay
        self.relays, self.arrivals = [], []

    def place(self, by_x, by_z):
        z_lo = self.z_lo if by_z == 0 else 1 - self.z_lo
        return step_to(self.x, by_x) * 2 + z_lo

    def start(self, by_x, by_z):
        own, there = self.place(0, 0), self.place(by_x, by_z)
        send = self.copies.send
        if by_x == 2:
            for half, by in ((0, 1), (1, 3)):
                copy = send(self.chunk(there, half), self.relay(by_z, half), self.device(self.place(by, by_z)))
                self.relays.append((copy, by_z, half))
        else:
            self.arrivals.append(send(self.chunk(there, None), self.landing(own, None), self.device(there)))

    def forward(self):
        for copy, by_z, half in self.relays:
            copy.wait_recv()
            came, by = ((3, 1), (1, 3))[half]
            target = self.landing(self.place(came, by_z), half)
            self.arrivals.append(
                self.copies.send(self.relay(by_z, half), target, self.device(self.place(by, 0)))
            )

    def arrive(self):
        for copy in self.arrivals:
            copy.wait_recv()


ORDER = ((2, 1), (2, 0), (1, 1), (3, 1), (1, 0), (3, 0), (0, 1), (0, 0))
TILES = 4


def front_kernel(
    ids, text_table, code_tables, temporal, context_weight, gain, gate_weight, up_weight, hidden, stream,
    normed_out, gate_out, up_out, gain_out, context_out, grid_out,
    table, staged, table_sems, picked,
    c_term, c_pass, c_direct, c_ended, c_pair, c_last, context,
    e_send, e_in, e_relay, g_send, g_relay,
    gate_w, up_w, hidden_in, stream_in, load_sems,
    normed, gate_back, up_back, out_sems, unit, scale, back, context_grad, gain_sum, send_sems, recv_sems,
):
    core, x, y, z = position()
    z_lo = lax.rem(z, 2)
    own = x * 2 + z_lo
    frames_all = temporal.shape[0]
    frames = frames_all // 8
    tile = frames // TILES
    rows = tile * 8
    half_rows = rows // 2
    seq = lax.axis_index("seq")
    device = lambda place: (seq, place)
    copies = Copies(send_sems, recv_sems)

    loads = []
    for at, (source, target) in enumerate(
        ((gate_weight, gate_w), (up_weight, up_w), (hidden, hidden_in), (stream, stream_in))
    ):
        loads.append(pltpu.make_async_copy(source, target, load_sems.at[at]))

    block = staged.shape[1]
    text_blocks = text_table.shape[0] // block
    blocks = table.shape[0] // block

    def load_block(i):
        source = text_table if i < text_blocks else code_tables
        first = (i if i < text_blocks else i - text_blocks) * block
        return pltpu.make_async_copy(
            source.at[pl.ds(first, block)], staged.at[i % 2], table_sems.at[i % 2]
        )

    block_loads = [load_block(i) for i in range(blocks)]
    block_loads[0].start()
    block_loads[1].start()
    for load in loads:
        load.start()
    greet([device(lax.rem(own + by, 8)) for by in range(1, 8)])

    def context_body(i, carry):
        block_rows = pl.ds(pl.multiple_of(i * frames, frames), frames)
        partial = jnp.dot(temporal[block_rows], context_weight[...], preferred_element_type=F32)
        c_term[lax.div(i, 2), lax.rem(i, 2)] = partial.astype(BF16)
        return carry

    lax.fori_loop(0, 8, context_body, 0)
    half_width = c_term.shape[-1] // 2
    c_half = lambda half: pl.ds(half * half_width, half_width)
    c_pick = lambda ref: lambda half: ref.at[:, :, c_half(half)]
    c_ring = Ring(
        copies, x, lambda at: device(at * 2 + z_lo),
        lambda at, half: c_term.at[at, :, :, c_half(half)],
        c_pick(c_pass), c_pick(c_direct), c_pick(c_ended),
    )
    c_ring.first()

    def add_context(out, refs):
        def body(i, carry):
            at = pl.ds(pl.multiple_of(lax.rem(i, frames // 16) * 16, 16), 16)
            low = lax.div(i, frames // 16)
            total = refs[0][low, at].astype(F32)
            for ref in refs[1:]:
                total = total + ref[low, at].astype(F32)
            out[low, at] = total.astype(BF16)
            return carry

        lax.fori_loop(0, frames // 8, body, 0)

    for i in range(blocks):
        block_loads[i].wait()

        def widen(j, carry):
            at = pl.multiple_of(j * 128, 128)
            table[pl.ds(i * block + at, 128)] = staged[i % 2, pl.ds(at, 128)].astype(F32)
            return carry

        lax.fori_loop(0, block // 128, widen, 0)
        if i + 2 < blocks:
            block_loads[i + 2].start()

    def gather(t, place, target):
        def body(f, carry):
            frame = place * frames + t * tile + f
            for k in range(8):
                picked[pl.ds(f * 8 + k, 1)] = table[pl.ds(ids[k * frames_all + frame], 1)]
            return carry

        lax.fori_loop(0, tile, body, 0, unroll=4)
        target[...] = picked[...].astype(BF16)

    def tile_rows(t, half):
        if half is None:
            return pl.ds(t * rows, rows)
        return pl.ds(t * rows + half * half_rows, half_rows)

    def exchange(t, send_ref, in_ref, relay_ref):
        return Exchange(
            copies, x, z_lo, device,
            lambda place, half: send_ref.at[place, tile_rows(t, half)],
            lambda place, half: in_ref.at[place, tile_rows(t, half)],
            lambda by_z, half: relay_ref.at[t, by_z, half],
        )

    rows_in = [exchange(t, e_send, e_in, e_relay) for t in range(TILES)]
    rows_back = [exchange(t, g_send, grid_out, g_relay) for t in range(TILES)]

    def gather_tile(t):
        for by_x, by_z in ORDER:
            place = rows_in[t].place(by_x, by_z)
            if (by_x, by_z) == (0, 0):
                gather(t, place, e_in.at[place, tile_rows(t, None)])
            else:
                gather(t, place, e_send.at[place, tile_rows(t, None)])
                rows_in[t].start(by_x, by_z)

    gather_tile(0)
    c_ring.second(add_context)
    gather_tile(1)
    rows_in[0].forward()
    c_ring.third(add_context, lambda half: c_pair.at[:, :, c_half(half)])
    c_copy = copies.send(c_pair.at[1 - z_lo], c_last, device(x * 2 + 1 - z_lo))
    gather_tile(2)
    rows_in[1].forward()
    gather_tile(3)
    rows_in[2].forward()
    c_copy.wait_recv()

    def context_total(i, carry):
        at = pl.ds(pl.multiple_of(i * 16, 16), 16)
        context[at] = c_pair[z_lo, at].astype(F32) + c_last[at].astype(F32)
        return carry

    lax.fori_loop(0, frames // 16, context_total, 0)

    width = context.shape[1]
    column_blocks = width // 128
    gain_sum[...] = jnp.zeros(gain_sum.shape, F32)
    for load in loads:
        load.wait()

    def run_tile(t):
        slot = t % 2
        rows_in[t].arrive()

        def norm(i, carry):
            first = t * rows + i * 32
            at = pl.ds(pl.multiple_of(i * 32, 32), 32)
            frame_rows = [
                context[pl.ds(t * tile + i * 4 + f, 1)] for f in range(4)
            ]
            spread = jnp.concatenate([jnp.broadcast_to(row, (8, width)) for row in frame_rows], axis=0)
            embedded = jnp.concatenate(
                [e_in[j, pl.ds(pl.multiple_of(first, 32), 32)] for j in range(column_blocks)], axis=1
            )
            depth = (spread + embedded.astype(F32)).astype(BF16).astype(F32)
            inv = lax.rsqrt(jnp.mean(depth * depth, axis=1, keepdims=True) + EPSILON)
            unit_rows = depth * inv
            unit[at] = unit_rows
            scale[at] = jnp.broadcast_to(inv, (32, 128))
            normed[slot, at] = (unit_rows * gain[...]).astype(BF16)
            return carry

        lax.fori_loop(0, rows // 32, norm, 0)

        def forward_pass(j, carry):
            columns = pl.ds(pl.multiple_of(j * 256, 256), 256)
            left = normed[slot]
            gate = jnp.dot(left, gate_w[:, columns], preferred_element_type=F32)
            up = jnp.dot(left, up_w[:, columns], preferred_element_type=F32)
            upstream = hidden_in[pl.ds(t * rows, rows), columns].astype(F32)
            sigma = jax.nn.sigmoid(gate)
            with_sigma = upstream * sigma
            gate_back[slot, :, columns] = (with_sigma * up * (1.0 + gate * (1.0 - sigma))).astype(BF16)
            up_back[slot, :, columns] = (with_sigma * gate).astype(BF16)
            return carry

        lax.fori_loop(0, gate_w.shape[1] // 256, forward_pass, 0)
        outs = [
            pltpu.make_async_copy(ref.at[slot], target.at[pl.ds(t * rows, rows)], out_sems.at[slot, n])
            for n, (ref, target) in enumerate(
                ((normed, normed_out), (gate_back, gate_out), (up_back, up_out))
            )
        ]
        for out in outs:
            out.start()

        transposed = (((1,), (1,)), ((), ()))

        def backward_pass(j, carry):
            columns = pl.ds(pl.multiple_of(j * 256, 256), 256)
            total = lax.dot_general(
                gate_back[slot], gate_w[columns], transposed, preferred_element_type=F32
            )
            total = total + lax.dot_general(
                up_back[slot], up_w[columns], transposed, preferred_element_type=F32
            )
            back[:, columns] = total
            return carry

        lax.fori_loop(0, width // 256, backward_pass, 0)

        def finish(i, carry):
            at = pl.ds(pl.multiple_of(i * 64, 64), 64)
            whole = pl.ds(pl.multiple_of(t * rows + i * 64, 64), 64)
            normed_back, unit_rows = back[at], unit[at]
            gain_sum[...] += jnp.sum((normed_back * unit_rows).reshape(8, 8, width), axis=0)
            scaled = normed_back * gain[...]
            mean = jnp.mean(scaled * unit_rows, axis=1, keepdims=True)
            depth = stream_in[whole].astype(F32) + scale[at, :1] * (scaled - unit_rows * mean)
            depth = depth.astype(BF16)
            for j in range(column_blocks):
                g_send[j, whole] = depth[:, j * 128 : (j + 1) * 128]
            frame_rows = pl.ds(pl.multiple_of(t * tile + i * 8, 8), 8)
            context_grad[frame_rows] = jnp.sum(depth.astype(F32).reshape(8, 8, width), axis=1)
            return carry

        lax.fori_loop(0, rows // 64, finish, 0)
        for by_x, by_z in ORDER[:-1]:
            rows_back[t].start(by_x, by_z)
        grid_out[own, pl.ds(t * rows, rows)] = g_send[own, pl.ds(t * rows, rows)]
        return outs

    outs = [run_tile(0)]
    rows_in[3].forward()
    outs.append(run_tile(1))
    rows_back[0].forward()
    for out in outs[0]:
        out.wait()
    outs.append(run_tile(2))
    rows_back[1].forward()
    for out in outs[1]:
        out.wait()
    outs.append(run_tile(3))
    rows_back[2].forward()
    context_out[...] = context_grad[...].astype(BF16)
    gain_row = jnp.sum(gain_sum[...], axis=0, keepdims=True)
    for j in range(8):
        gain_out[j : j + 1] = gain_row[:, j * 128 : (j + 1) * 128]
    rows_back[3].forward()
    for out in outs[2] + outs[3]:
        out.wait()
    for t in range(TILES):
        rows_back[t].arrive()
    copies.finish()


def front(ids, text_table, code_tables, temporal, context_weight, gain, gate_weight, up_weight, hidden, stream):
    frames_all = temporal.shape[0]
    frames = frames_all // 8
    width, hidden_width = gate_weight.shape
    rows = frames * 8 // TILES
    bf = lambda *shape: pltpu.VMEM(shape, BF16)
    f32 = lambda *shape: pltpu.VMEM(shape, F32)
    dma = lambda *shape: pltpu.SemaphoreType.DMA(shape)
    vmem = pl.BlockSpec(memory_space=pltpu.VMEM)
    anywhere = pl.BlockSpec(memory_space=pl.ANY)
    table_rows = text_table.shape[0] + code_tables.shape[0]
    return pl.pallas_call(
        front_kernel,
        out_shape=(
            jax.ShapeDtypeStruct((frames * 8, width), BF16),
            jax.ShapeDtypeStruct((frames * 8, hidden_width), BF16),
            jax.ShapeDtypeStruct((frames * 8, hidden_width), BF16),
            jax.ShapeDtypeStruct((8, width // 8), F32),
            jax.ShapeDtypeStruct((frames, width), BF16),
            jax.ShapeDtypeStruct((8, frames * 8, 128), BF16),
        ),
        in_specs=[pl.BlockSpec(memory_space=pltpu.SMEM), anywhere, anywhere, vmem, vmem, vmem]
        + [anywhere] * 4,
        out_specs=(anywhere, anywhere, anywhere, vmem, vmem, vmem),
        scratch_shapes=[
            f32(table_rows, 128), bf(2, 2048, 128), dma(2), f32(rows, 128),
            bf(4, 2, frames, width), bf(2, frames, width), bf(2, frames, width), bf(2, frames, width),
            bf(2, frames, width), bf(frames, width), f32(frames, width),
            bf(8, frames * 8, 128), bf(8, frames * 8, 128), bf(TILES, 2, 2, rows // 2, 128),
            bf(8, frames * 8, 128), bf(TILES, 2, 2, rows // 2, 128),
            bf(width, hidden_width), bf(width, hidden_width),
            bf(frames * 8, hidden_width), bf(frames * 8, width), dma(4),
            bf(2, rows, width), bf(2, rows, hidden_width), bf(2, rows, hidden_width), dma(2, 3),
            f32(rows, width), f32(rows, 128), f32(rows, width), f32(frames, width), f32(8, width),
            dma(120), dma(120),
        ],
        compiler_params=pltpu.CompilerParams(
            collective_id=2, has_side_effects=True, vmem_limit_bytes=VMEM_LIMIT
        ),
        cost_estimate=pl.CostEstimate(
            flops=19_000_000_000, bytes_accessed=40_000_000, transcendentals=2_000_000
        ),
        name="front",
    )(ids, text_table, code_tables, temporal, context_weight, gain, gate_weight, up_weight, hidden, stream)


CHUNKS = 3


def total_of(refs):
    total = refs[0][...].astype(F32)
    for ref in refs[1:]:
        total = total + ref[...].astype(F32)
    return total


def add_into(out, refs):
    out[...] = total_of(refs).astype(BF16)


def reduce_kernel(
    normed, gate_back, up_back, gain, tables,
    weight_out, gain_out, table_mine, table_last,
    left_in, gate_in, up_in, turned, term, pair,
    x_bufs, x_sums, xz_bufs, z_bufs, z_sums, zx_bufs, y_term, y_bufs,
    own, other, t_bufs, t_sum, t_relay, gain_own, gain_in,
    local_sems, send_sems, recv_sems,
):
    core, x, y, z = position()
    quarter = term.shape[-1] // 4
    table_rows = own.shape[2]
    chunk_rows = table_rows // CHUNKS
    half_rows = chunk_rows // 2
    z_hi = lax.div(z, 2)
    sibling = device_at(1 - core, x, y, z)
    x_device = lambda at: device_at(core, at, y, z)
    y_device = lambda at: device_at(core, x, at, z)
    z_device = lambda at: device_at(core, x, y, at)
    t_rows = lambda c: pl.ds(c * chunk_rows, chunk_rows)
    keeps = [
        pltpu.make_async_copy(tables.at[core, :, :, t_rows(c)], own.at[:, :, t_rows(c)], local_sems.at[c])
        for c in range(CHUNKS)
    ]
    loads = [
        pltpu.make_async_copy(source, target, local_sems.at[CHUNKS + n])
        for n, (source, target) in enumerate(
            ((normed, left_in), (gate_back, gate_in), (up_back, up_in))
        )
    ]
    for load in loads + keeps:
        load.start()
    greet(
        [sibling]
        + [x_device(step_to(x, by)) for by in (1, 2, 3)]
        + [y_device(step_to(y, by)) for by in (1, 2, 3)]
        + [z_device(step_to(z, by)) for by in (1, 2, 3)]
    )
    copies = Copies(send_sems, recv_sems)

    table_pairs = [
        [
            copies.send(tables.at[1 - core, i, :, t_rows(c)], other.at[i, :, t_rows(c)], sibling)
            for i in range(4)
        ]
        for c in range(CHUNKS)
    ]
    gain_own[0] = gain[...]
    gain_copy = copies.send(gain_own.at[0], gain_in.at[0], sibling)

    def make_term(q):
        turned[:128] = left_in[:, q * 128 : (q + 1) * 128].T
        turned[128:] = left_in[:, (q + 4) * 128 : (q + 5) * 128].T

        def body(i, carry):
            columns = pl.ds(pl.multiple_of(i * 256, 256), 256)
            left = turned[...]
            gate = jnp.dot(left, gate_in[:, columns], preferred_element_type=F32)
            up = jnp.dot(left, up_in[:, columns], preferred_element_type=F32)
            both = jnp.concatenate([gate.reshape(32, 8, 256), up.reshape(32, 8, 256)], axis=1)
            both = both.astype(BF16).reshape(2, 2, 4, 2, 16, 256)
            for hi in range(2):
                term[:, q, :, pl.ds(hi * 2, 2), :, columns] = both[hi]
            return carry

        lax.fori_loop(0, gate_in.shape[1] // 256, body, 0)

    pair_copies = []

    def send_pair(q):
        pair_copies.append(copies.send(term.at[1 - core, q], pair.at[q], sibling))

    def add_pair(q):
        pair_copies[q].wait_recv()

        def body(i, carry):
            column, depth = lax.div(i, 4), lax.rem(i, 4)
            total = term[core, q, column, depth].astype(F32) + pair[q, column, depth].astype(F32)
            term[core, q, column, depth] = total.astype(BF16)
            return carry

        lax.fori_loop(0, 16, body, 0)

    x_half = lambda half: pl.ds(half * quarter, quarter)
    z_half = lambda half: pl.ds((half + 2) * quarter, quarter)

    def make_ring(here, device, part, bufs, q):
        picks = [
            lambda half, n=n: bufs.at[(n, q) + (slice(None),) * (len(bufs.shape) - 3) + (x_half(half),)]
            for n in range(3)
        ]
        return Ring(copies, here, device, part, *picks)

    first_rings = [
        (
            make_ring(x, x_device, lambda at, half, q=q: term.at[core, q, at, :, :, x_half(half)], x_bufs, q),
            make_ring(z, z_device, lambda at, half, q=q: term.at[core, q, :, at, :, z_half(half)], z_bufs, q),
        )
        for q in range(4)
    ]
    second_rings = [
        (
            make_ring(z, z_device, lambda at, half, q=q: x_sums.at[q, at, :, x_half(half)], xz_bufs, q),
            make_ring(x, x_device, lambda at, half, q=q: z_sums.at[q, at, :, x_half(half)], zx_bufs, q),
        )
        for q in range(4)
    ]

    def first_out(q):
        first_rings[q][0].third(add_into, lambda half: x_sums.at[q, :, :, x_half(half)])
        first_rings[q][1].third(add_into, lambda half: z_sums.at[q, :, :, x_half(half)])
        for ring in second_rings[q]:
            ring.first()

    def second_out(q):
        second_rings[q][0].third(add_into, lambda half: y_term.at[q, :, x_half(half)])
        second_rings[q][1].third(add_into, lambda half: y_term.at[q, :, z_half(half)])

    def first_start(q):
        add_pair(q)
        for ring in first_rings[q]:
            ring.first()

    def first_middle(q):
        for ring in first_rings[q]:
            ring.second(add_into)

    def second_middle(q):
        for ring in second_rings[q]:
            ring.second(add_into)

    t_half = lambda c, half: pl.ds(c * chunk_rows + half * half_rows, half_rows)
    t_rings = [
        Ring(
            copies, y, y_device,
            lambda at, half, c=c: own.at[at, :, t_half(c, half)],
            *(lambda half, n=n, c=c: t_bufs.at[n, :, t_half(c, half)] for n in range(3)),
        )
        for c in range(CHUNKS)
    ]

    def add_tables(out, refs):
        def body(i, carry):
            rows = pl.ds(pl.multiple_of(i * 64, 64), 64)
            for hi in range(2):
                out[hi, rows] = total_of([ref.at[hi, rows] for ref in refs]).astype(BF16)
            return carry

        lax.fori_loop(0, half_rows // 64, body, 0)

    def pair_tables(c):
        keeps[c].wait()
        for copy in table_pairs[c]:
            copy.wait_recv()

        def body(i, carry):
            rows = pl.ds(pl.multiple_of(c * chunk_rows + lax.rem(i, chunk_rows // 128) * 128, 128), 128)
            at = lax.div(i, chunk_rows // 128)
            for hi in range(2):
                own[at, hi, rows] = total_of([own.at[at, hi, rows], other.at[at, hi, rows]]).astype(BF16)
            return carry

        lax.fori_loop(0, 4 * (chunk_rows // 128), body, 0)
        t_rings[c].first()

    t_relays, t_arrivals = {}, []

    def tables_out(c):
        t_rings[c].third(add_tables, lambda half: t_sum.at[:, t_half(c, half)])
        t_relays[c] = [
            copies.send(t_sum.at[1 - z_hi, t_half(c, half)], t_relay.at[t_half(c, half)], z_device(step_to(z, by)))
            for half, by in ((0, 1), (1, 3))
        ]

    def tables_relay(c):
        for copy, half, by in zip(t_relays[c], (0, 1), (1, 3)):
            copy.wait_recv()
            rows = t_half(c, half)
            t_arrivals.append(copies.send(t_relay.at[rows], table_last.at[rows], z_device(step_to(z, by))))

    def gain_round(index, device, here):
        gain_own[index] = gain_own[index - 1] + gain_sum
        return [
            copies.send(gain_own.at[index], gain_in.at[index * 3 + by - 3], device(step_to(here, by)))
            for by in (1, 2, 3)
        ]

    def gain_total(waited, slots):
        for copy in waited:
            copy.wait_recv()
        total = gain_in[slots[0]]
        for slot in slots[1:]:
            total = total + gain_in[slot]
        return total

    for load in loads:
        load.wait()
    make_term(0)
    send_pair(0)
    pair_tables(0)
    pair_tables(1)
    make_term(1)
    send_pair(1)
    pair_tables(2)
    first_start(0)
    t_rings[0].second(add_tables)
    gain_sum = gain_total([gain_copy], [0])
    gain_copies = gain_round(1, x_device, x)
    make_term(2)
    send_pair(2)
    first_start(1)
    first_middle(0)
    t_rings[1].second(add_tables)
    make_term(3)
    send_pair(3)
    first_start(2)
    first_middle(1)
    first_out(0)
    gain_sum = gain_total(gain_copies, [1, 2, 3])
    gain_copies = gain_round(2, y_device, y)
    first_start(3)
    first_middle(2)
    first_out(1)
    second_middle(0)
    t_rings[2].second(add_tables)
    tables_out(0)
    first_middle(3)
    first_out(2)
    second_middle(1)
    second_out(0)
    tables_out(1)
    tables_relay(0)
    gain_sum = gain_total(gain_copies, [4, 5, 6])
    gain_copies = gain_round(3, z_device, z)
    first_out(3)
    second_middle(2)
    second_out(1)
    tables_relay(1)
    tables_out(2)
    second_middle(3)
    second_out(2)
    second_out(3)

    y_half = lambda half: pl.ds(half * 2 * quarter, 2 * quarter)
    y_ring = Ring(
        copies, y, y_device,
        lambda at, half: y_term.at[at, :, y_half(half)],
        *(lambda half, n=n: y_bufs.at[n, :, y_half(half)] for n in range(3)),
    )
    y_ring.first()
    tables_relay(2)
    gain_out[...] = gain_own[3] + gain_total(gain_copies, [7, 8, 9])
    y_ring.second(add_into)

    def copy_mine(i, carry):
        rows = pl.ds(pl.multiple_of(i * 128, 128), 128)
        table_mine[rows] = t_sum[z_hi, rows]
        return carry

    lax.fori_loop(0, table_rows // 128, copy_mine, 0)

    def finish_weights(out, refs):
        weight_out[:, out] = total_of(refs)

    y_ring.third(finish_weights, y_half)
    for copy in t_arrivals:
        copy.wait_recv()
    copies.finish()


def reduce_all(normed, gate_back, up_back, gain_part, tables):
    rows, features = normed.shape
    width = gate_back.shape[1]
    table_rows = tables.shape[3]
    bf = lambda *shape: pltpu.VMEM(shape, BF16)
    vmem = pl.BlockSpec(memory_space=pltpu.VMEM)
    anywhere = pl.BlockSpec(memory_space=pl.ANY)
    return pl.pallas_call(
        reduce_kernel,
        out_shape=(
            jax.ShapeDtypeStruct((16, width), F32),
            jax.ShapeDtypeStruct((8, 128), F32),
            jax.ShapeDtypeStruct((table_rows, 128), BF16),
            jax.ShapeDtypeStruct((table_rows, 128), BF16),
        ),
        in_specs=[anywhere, anywhere, anywhere, vmem, anywhere],
        out_specs=(vmem,) * 4,
        scratch_shapes=[
            bf(rows, features), bf(rows, width), bf(rows, width), bf(256, rows),
            bf(2, 4, 4, 4, 16, width), bf(4, 4, 4, 16, width),
            bf(3, 4, 4, 16, width // 2), bf(4, 4, 16, width // 2), bf(3, 4, 16, width // 2),
            bf(3, 4, 4, 16, width // 2), bf(4, 4, 16, width // 2), bf(3, 4, 16, width // 2),
            bf(4, 16, width), bf(3, 16, width),
            bf(4, 2, table_rows, 128), bf(4, 2, table_rows, 128), bf(3, 2, table_rows, 128),
            bf(2, table_rows, 128), bf(table_rows, 128),
            pltpu.VMEM((4, 8, 128), F32), pltpu.VMEM((10, 8, 128), F32),
            pltpu.SemaphoreType.DMA((CHUNKS + 3,)),
            pltpu.SemaphoreType.DMA((160,)),
            pltpu.SemaphoreType.DMA((160,)),
        ],
        compiler_params=pltpu.CompilerParams(
            collective_id=1, has_side_effects=True, vmem_limit_bytes=VMEM_LIMIT
        ),
        cost_estimate=pl.CostEstimate(flops=9_000_000_000, bytes_accessed=20_000_000, transcendentals=0),
        name="reduce_all",
    )(normed, gate_back, up_back, gain_part, tables)


def results_kernel(weights, mine, last, gate_out, up_out, text_out, code_out):
    gate_out[...] = weights[:8]
    up_out[...] = weights[8:]
    text_rows = text_out.shape[0]

    def text_body(i, carry):
        rows = pl.ds(pl.multiple_of(i * 128, 128), 128)
        text_out[rows] = mine[rows].astype(F32) + last[rows].astype(F32)
        return carry

    lax.fori_loop(0, text_rows // 128, text_body, 0)
    for c in range(code_out.shape[0]):
        rows = pl.ds(text_rows + c * code_out.shape[1], code_out.shape[1])
        code_out[c] = mine[rows].astype(F32) + last[rows].astype(F32)


def results(weights, mine, last, text_rows, codes):
    vmem = pl.BlockSpec(memory_space=pltpu.VMEM)
    code_rows = (mine.shape[0] - text_rows) // codes
    return pl.pallas_call(
        results_kernel,
        out_shape=(
            jax.ShapeDtypeStruct((8, weights.shape[1]), F32),
            jax.ShapeDtypeStruct((8, weights.shape[1]), F32),
            jax.ShapeDtypeStruct((text_rows, 128), F32),
            jax.ShapeDtypeStruct((codes, code_rows, 128), F32),
        ),
        in_specs=[vmem] * 3,
        out_specs=(vmem,) * 4,
        compiler_params=pltpu.CompilerParams(vmem_limit_bytes=VMEM_LIMIT),
        name="results",
    )(weights, mine, last)


def scatter_kernel(ids, grads, tables, rows, total, text_count, card, codes):
    frames = grads.shape[0]
    count = total.shape[0]

    def clear(i, carry):
        total[pl.ds(pl.multiple_of(i * 256, 256), 256)] = jnp.zeros((256, 128), F32)
        return carry

    lax.fori_loop(0, count // 256, clear, 0)

    def widen(i, carry):
        block = grads[pl.ds(i * 16, 16)].astype(F32).reshape(128, 128)
        rows[pl.ds(pl.multiple_of(i * 128, 128), 128)] = block
        return carry

    lax.fori_loop(0, frames // 16, widen, 0)

    def body(f, carry):
        places = [ids[k * frames + f] for k in range(codes + 1)]
        sums = [
            total[pl.ds(places[k], 1)] + rows[pl.ds(f * (codes + 1) + k, 1)]
            for k in range(codes + 1)
        ]
        for k in range(codes + 1):
            total[pl.ds(places[k], 1)] = sums[k]
        return carry

    lax.fori_loop(0, frames, body, 0, unroll=4)

    text_block, code_block = text_count // 16, card // 16
    for block in range(16):
        z_hi, y, core = block // 8, block // 2 % 4, block % 2
        tables[core, y, z_hi, :text_block] = total[
            block * text_block : (block + 1) * text_block
        ].astype(BF16)
        for c in range(codes):
            first = text_count + c * card + block * code_block
            tables[core, y, z_hi, pl.ds(text_block + c * code_block, code_block)] = total[
                first : first + code_block
            ].astype(BF16)


def scatter_rows(ids, grads, text_count, card, codes):
    rows = text_count // 16 + codes * card // 16
    return pl.pallas_call(
        functools.partial(scatter_kernel, text_count=text_count, card=card, codes=codes),
        out_shape=jax.ShapeDtypeStruct((2, 4, 2, rows, 128), BF16),
        in_specs=[pl.BlockSpec(memory_space=pltpu.SMEM), pl.BlockSpec(memory_space=pltpu.VMEM)],
        out_specs=pl.BlockSpec(memory_space=pltpu.VMEM),
        scratch_shapes=[
            pltpu.VMEM((grads.shape[0] * (codes + 1), 128), F32),
            pltpu.VMEM((text_count + codes * card, 128), F32),
        ],
        compiler_params=pltpu.CompilerParams(vmem_limit_bytes=VMEM_LIMIT),
        name="scatter_rows",
    )(ids, grads)


def on_device(
    temporal_out,
    context_weight,
    text_ids,
    code_ids,
    text_table,
    code_tables,
    norm_gain,
    gate_weight,
    up_weight,
    hidden_grad,
    stream_grad,
):
    code_count, card_size, feature_width = code_tables.shape
    text_count = text_table.shape[0]
    code_offsets = jnp.arange(code_count, dtype=jnp.int32)[:, None] * card_size + text_count
    places = jnp.concatenate([text_ids[None], code_ids.T + code_offsets], axis=0).reshape(-1)
    normed, gate_back, up_back, gain_part, context_grad, grid = front(
        places,
        text_table,
        code_tables.reshape(code_count * card_size, feature_width),
        temporal_out,
        context_weight,
        norm_gain.reshape(1, -1),
        gate_weight,
        up_weight,
        hidden_grad.reshape(-1, hidden_grad.shape[2]),
        stream_grad.reshape(-1, stream_grad.shape[2]),
    )
    tables = scatter_rows(places, grid.reshape(-1, 8, feature_width), text_count, card_size, code_count)
    weights, gain_sum, mine, last = reduce_all(normed, gate_back, up_back, gain_part, tables)
    gate_grad, up_grad, text_grad, code_grad = results(
        weights, mine, last, text_count // lax.axis_size("seq"), code_count
    )
    own_place = lax.axis_index("seq") * lax.axis_size("tp") + lax.axis_index("tp")
    gain_grad = lax.dynamic_slice_in_dim(gain_sum.reshape(-1), own_place * 8, 8)
    return (gate_grad, up_grad, gain_grad, text_grad, code_grad, context_grad)


def solution(mesh):
    return jax.shard_map(
        on_device,
        mesh=mesh,
        in_specs=(
            P("seq", "tp"),
            P("tp", None),
            P("seq"),
            P("seq", None),
            P(None, "tp"),
            P(None, None, "tp"),
            P(),
            P(),
            P(),
            P(("seq", "tp"), None, None),
            P(("seq", "tp"), None, None),
        ),
        out_specs=(
            P(("seq", "tp"), None),
            P(("seq", "tp"), None),
            P(("seq", "tp")),
            P("seq", "tp"),
            P(None, "seq", "tp"),
            P(("seq", "tp"), None),
        ),
        check_vma=False,
    )
```

```python
import functools

import jax
import jax.numpy as jnp
from jax import lax
from jax.experimental import pallas as pl
from jax.experimental.pallas import tpu as pltpu
from jax.sharding import PartitionSpec as P

EPSILON = 1e-05

MESH = pl.DeviceIdType.MESH
F32 = jnp.float32
BF16 = jnp.bfloat16
VMEM_LIMIT = 60 * 1024 * 1024


def position():
    seq = lax.axis_index("seq")
    tp = lax.axis_index("tp")
    core = lax.rem(seq, 2)
    y = lax.rem(lax.div(seq, 2), 4)
    z_hi = lax.div(seq, 8)
    x = lax.div(tp, 2)
    z_lo = lax.rem(tp, 2)
    return core, x, y, z_hi * 2 + z_lo


def device_at(core, x, y, z):
    seq = (lax.div(z, 2) * 4 + y) * 2 + core
    tp = x * 2 + lax.rem(z, 2)
    return (seq, tp)


def step_to(value, by):
    return lax.rem(value + by, 4)


def greet(devices):
    for device in devices:
        pl.semaphore_signal(
            pltpu.get_barrier_semaphore(), inc=1, device_id=device, device_id_type=MESH
        )


def greeted(devices):
    pl.semaphore_wait(pltpu.get_barrier_semaphore(), len(devices))


class Copies:
    def __init__(self, send_sems, recv_sems):
        self.send_sems, self.recv_sems, self.made = send_sems, recv_sems, []

    def send(self, source, target, device):
        at = len(self.made)
        copy = pltpu.make_async_remote_copy(
            src_ref=source,
            dst_ref=target,
            send_sem=self.send_sems.at[at],
            recv_sem=self.recv_sems.at[at],
            device_id=device,
            device_id_type=MESH,
        )
        copy.start()
        self.made.append(copy)
        return copy

    def finish(self):
        for copy in self.made:
            copy.wait_send()


class Ring:
    def __init__(self, copies, here, device, part, pass_on, direct, ended):
        self.copies, self.here, self.device, self.part = copies, here, device, part
        self.pass_on, self.direct, self.ended = pass_on, direct, ended

    def first(self):
        for by in (2, 1, 3):
            self.first_to(by)

    def first_to(self, by):
        there = step_to(self.here, by)
        up_device, down_device = (self.device(step_to(self.here, to)) for to in (1, 3))
        send = self.copies.send
        if by == 2:
            self.from_down = send(self.part(there, 0), self.pass_on(0), up_device)
            self.from_up = send(self.part(there, 1), self.pass_on(1), down_device)
        elif by == 1:
            self.near = [send(self.part(there, 1), self.direct(1), up_device)]
        else:
            self.near.append(send(self.part(there, 0), self.direct(0), down_device))

    def second(self, add):
        up, down = step_to(self.here, 1), step_to(self.here, 3)
        self.from_down.wait_recv()
        add(self.part(up, 0), [self.part(up, 0), self.pass_on(0)])
        last_up = self.copies.send(self.part(up, 0), self.ended(0), self.device(up))
        self.from_up.wait_recv()
        add(self.part(down, 1), [self.part(down, 1), self.pass_on(1)])
        last_down = self.copies.send(self.part(down, 1), self.ended(1), self.device(down))
        self.last = [last_up, last_down]

    def third(self, add, out):
        for copy in self.near + self.last:
            copy.wait_recv()
        for half in (0, 1):
            add(out(half), [self.part(self.here, half), self.direct(half), self.ended(half)])


class Exchange:
    def __init__(self, copies, x, z_lo, device, chunk, landing):
        self.copies, self.x, self.z_lo, self.device = copies, x, z_lo, device
        self.chunk, self.landing, self.arrivals = chunk, landing, []

    def place(self, by_x, by_z):
        z_lo = self.z_lo if by_z == 0 else 1 - self.z_lo
        return step_to(self.x, by_x) * 2 + z_lo

    def start(self, by_x, by_z):
        own, there = self.place(0, 0), self.place(by_x, by_z)
        self.arrivals.append(
            self.copies.send(self.chunk(there), self.landing(own), self.device(there))
        )

    def arrive(self):
        for copy in self.arrivals:
            copy.wait_recv()


ORDER = ((2, 1), (2, 0), (1, 1), (3, 1), (1, 0), (3, 0), (0, 1), (0, 0))
TILES = 4


def front_kernel(
    ids, text_table, code_tables, temporal, context_weight, gain, gate_weight, up_weight, hidden, stream,
    normed_out, gate_out, up_out, gain_out, context_out, grid_out,
    table, staged, table_sems, picked,
    c_term, c_pass, c_direct, c_ended, c_pair, c_last, context,
    e_send, e_in, g_send,
    gate_w, up_w, hidden_in, stream_in, load_sems,
    normed, gate_back, up_back, out_sems, unit, scale, back, context_grad, gain_sum, send_sems, recv_sems,
):
    core, x, y, z = position()
    z_lo = lax.rem(z, 2)
    own = x * 2 + z_lo
    frames_all = temporal.shape[0]
    frames = frames_all // 8
    tile = frames // TILES
    rows = tile * 8
    seq = lax.axis_index("seq")
    device = lambda place: (seq, place)
    copies = Copies(send_sems, recv_sems)

    loads = []
    for at, (source, target) in enumerate(
        ((gate_weight, gate_w), (up_weight, up_w), (hidden, hidden_in), (stream, stream_in))
    ):
        loads.append(pltpu.make_async_copy(source, target, load_sems.at[at]))

    block = staged.shape[1]
    text_blocks = text_table.shape[0] // block
    blocks = table.shape[0] // block
    depth = staged.shape[0]

    def load_block(i):
        source = text_table if i < text_blocks else code_tables
        first = (i if i < text_blocks else i - text_blocks) * block
        return pltpu.make_async_copy(
            source.at[pl.ds(first, block)], staged.at[i % depth], table_sems.at[i % depth]
        )

    block_loads = [load_block(i) for i in range(blocks)]
    for i in range(depth):
        block_loads[i].start()
    others = [device(lax.rem(own + by, 8)) for by in range(1, 8)]
    greet(others)

    def context_part(at):
        def body(low, carry):
            block_rows = pl.ds(pl.multiple_of((at * 2 + low) * frames, frames), frames)
            partial = jnp.dot(temporal[block_rows], context_weight[...], preferred_element_type=F32)
            c_term[at, low] = partial.astype(BF16)
            return carry

        lax.fori_loop(0, 2, body, 0)

    half_width = c_term.shape[-1] // 2
    half_frames = frames // 2
    c_half = lambda half: pl.ds(half * half_width, half_width)
    c_frames = [pl.ds(h * half_frames, half_frames) for h in range(2)]

    def context_ring(h):
        pick = lambda ref: lambda half: ref.at[:, c_frames[h], c_half(half)]
        return Ring(
            copies, x, lambda at: device(at * 2 + z_lo),
            lambda at, half: c_term.at[at, :, c_frames[h], c_half(half)],
            pick(c_pass), pick(c_direct), pick(c_ended),
        )

    c_rings = [context_ring(h) for h in range(2)]

    def add_context(out, refs):
        def body(i, carry):
            at = pl.ds(pl.multiple_of(lax.rem(i, half_frames // 16) * 16, 16), 16)
            low = lax.div(i, half_frames // 16)
            out[low, at] = total_of([ref.at[low, at] for ref in refs]).astype(BF16)
            return carry

        lax.fori_loop(0, frames // 16, body, 0)

    def context_pair(h):
        c_rings[h].third(add_context, lambda half: c_pair.at[:, c_frames[h], c_half(half)])
        there = device(x * 2 + 1 - z_lo)
        return copies.send(c_pair.at[1 - z_lo, c_frames[h]], c_last.at[c_frames[h]], there)

    def context_total(h, copy):
        copy.wait_recv()

        def body(i, carry):
            at = pl.ds(pl.multiple_of(h * half_frames + i * 16, 16), 16)
            context[at] = total_of([c_pair.at[z_lo, at], c_last.at[at]])
            return carry

        lax.fori_loop(0, half_frames // 16, body, 0)

    context_part(step_to(x, 2))
    greeted(others)
    for by in (2, 1, 3):
        c_rings[0].first_to(by)
        context_part(step_to(x, {2: 1, 1: 3, 3: 0}[by]))

    for i in range(blocks):
        block_loads[i].wait()

        def widen(j, carry):
            at = pl.multiple_of(j * 128, 128)
            table[pl.ds(i * block + at, 128)] = staged[i % depth, pl.ds(at, 128)].astype(F32)
            return carry

        lax.fori_loop(0, block // 128, widen, 0)
        if i + depth < blocks:
            block_loads[i + depth].start()
        if i == blocks - depth:
            for load in loads:
                load.start()

    def gather(t, place, target):
        def body(f, carry):
            frame = place * frames + t * tile + f
            for k in range(8):
                picked[pl.ds(f * 8 + k, 1)] = table[pl.ds(ids[k * frames_all + frame], 1)]
            return carry

        lax.fori_loop(0, tile, body, 0, unroll=4)
        target[...] = picked[...].astype(BF16)

    def tile_rows(t):
        return pl.ds(t * rows, rows)

    def exchange(t, send_ref, in_ref):
        return Exchange(
            copies, x, z_lo, device,
            lambda place: send_ref.at[place, tile_rows(t)],
            lambda place: in_ref.at[place, tile_rows(t)],
        )

    rows_in = [exchange(t, e_send, e_in) for t in range(TILES)]
    rows_back = [exchange(t, g_send, grid_out) for t in range(TILES)]

    def gather_tile(t):
        for by_x, by_z in ORDER:
            place = rows_in[t].place(by_x, by_z)
            if (by_x, by_z) == (0, 0):
                gather(t, place, e_in.at[place, tile_rows(t)])
            else:
                gather(t, place, e_send.at[place, tile_rows(t)])

    def send_tile(t):
        for by_x, by_z in ORDER[:-1]:
            rows_in[t].start(by_x, by_z)

    gather_tile(0)
    c_rings[0].second(add_context)
    send_tile(0)
    c_rings[1].first()
    gather_tile(1)
    c_copy = context_pair(0)
    send_tile(1)
    gather_tile(2)
    c_rings[1].second(add_context)
    send_tile(2)
    gather_tile(3)
    context_total(0, c_copy)

    width = context.shape[1]
    column_blocks = width // 128
    gain_sum[...] = jnp.zeros(gain_sum.shape, F32)
    for load in loads:
        load.wait()

    def run_tile(t):
        slot = t % 2
        rows_in[t].arrive()

        def norm(i, carry):
            first = t * rows + i * 32
            at = pl.ds(pl.multiple_of(i * 32, 32), 32)
            frame_rows = [
                context[pl.ds(t * tile + i * 4 + f, 1)] for f in range(4)
            ]
            spread = jnp.concatenate([jnp.broadcast_to(row, (8, width)) for row in frame_rows], axis=0)
            embedded = jnp.concatenate(
                [e_in[j, pl.ds(pl.multiple_of(first, 32), 32)] for j in range(column_blocks)], axis=1
            )
            depth = (spread + embedded.astype(F32)).astype(BF16).astype(F32)
            inv = lax.rsqrt(jnp.mean(depth * depth, axis=1, keepdims=True) + EPSILON)
            unit_rows = depth * inv
            unit[at] = unit_rows
            scale[at] = jnp.broadcast_to(inv, (32, 128))
            normed[slot, at] = (unit_rows * gain[...]).astype(BF16)
            return carry

        lax.fori_loop(0, rows // 32, norm, 0)

        def forward_pass(j, carry):
            columns = pl.ds(pl.multiple_of(j * 256, 256), 256)
            left = normed[slot]
            gate = jnp.dot(left, gate_w[:, columns], preferred_element_type=F32)
            up = jnp.dot(left, up_w[:, columns], preferred_element_type=F32)
            upstream = hidden_in[pl.ds(t * rows, rows), columns].astype(F32)
            sigma = jax.nn.sigmoid(gate)
            with_sigma = upstream * sigma
            gate_back[slot, :, columns] = (with_sigma * up * (1.0 + gate * (1.0 - sigma))).astype(BF16)
            up_back[slot, :, columns] = (with_sigma * gate).astype(BF16)
            return carry

        lax.fori_loop(0, gate_w.shape[1] // 256, forward_pass, 0)
        outs = [
            pltpu.make_async_copy(ref.at[slot], target.at[pl.ds(t * rows, rows)], out_sems.at[slot, n])
            for n, (ref, target) in enumerate(
                ((normed, normed_out), (gate_back, gate_out), (up_back, up_out))
            )
        ]
        for out in outs:
            out.start()

        transposed = (((1,), (1,)), ((), ()))

        def backward_pass(j, carry):
            columns = pl.ds(pl.multiple_of(j * 256, 256), 256)
            total = lax.dot_general(
                gate_back[slot], gate_w[columns], transposed, preferred_element_type=F32
            )
            total = total + lax.dot_general(
                up_back[slot], up_w[columns], transposed, preferred_element_type=F32
            )
            back[:, columns] = total
            return carry

        lax.fori_loop(0, width // 256, backward_pass, 0)

        def finish(i, carry):
            at = pl.ds(pl.multiple_of(i * 64, 64), 64)
            whole = pl.ds(pl.multiple_of(t * rows + i * 64, 64), 64)
            normed_back, unit_rows = back[at], unit[at]
            gain_sum[...] += jnp.sum((normed_back * unit_rows).reshape(8, 8, width), axis=0)
            scaled = normed_back * gain[...]
            mean = jnp.mean(scaled * unit_rows, axis=1, keepdims=True)
            depth = stream_in[whole].astype(F32) + scale[at, :1] * (scaled - unit_rows * mean)
            depth = depth.astype(BF16)
            for j in range(column_blocks):
                g_send[j, whole] = depth[:, j * 128 : (j + 1) * 128]
            frame_rows = pl.ds(pl.multiple_of(t * tile + i * 8, 8), 8)
            context_grad[frame_rows] = jnp.sum(depth.astype(F32).reshape(8, 8, width), axis=1)
            return carry

        lax.fori_loop(0, rows // 64, finish, 0)
        for by_x, by_z in ORDER[:-1]:
            rows_back[t].start(by_x, by_z)
        grid_out[own, pl.ds(t * rows, rows)] = g_send[own, pl.ds(t * rows, rows)]
        return outs

    outs = [run_tile(0)]
    c_copy = context_pair(1)
    send_tile(3)
    outs.append(run_tile(1))
    for out in outs[0]:
        out.wait()
    context_total(1, c_copy)
    outs.append(run_tile(2))
    for out in outs[1]:
        out.wait()
    outs.append(run_tile(3))
    context_out[...] = context_grad[...].astype(BF16)
    gain_row = jnp.sum(gain_sum[...], axis=0, keepdims=True)
    for j in range(8):
        gain_out[j : j + 1] = gain_row[:, j * 128 : (j + 1) * 128]
    for out in outs[2] + outs[3]:
        out.wait()
    for t in range(TILES):
        rows_back[t].arrive()
    copies.finish()


def front(ids, text_table, code_tables, temporal, context_weight, gain, gate_weight, up_weight, hidden, stream):
    frames_all = temporal.shape[0]
    frames = frames_all // 8
    width, hidden_width = gate_weight.shape
    rows = frames * 8 // TILES
    bf = lambda *shape: pltpu.VMEM(shape, BF16)
    f32 = lambda *shape: pltpu.VMEM(shape, F32)
    dma = lambda *shape: pltpu.SemaphoreType.DMA(shape)
    vmem = pl.BlockSpec(memory_space=pltpu.VMEM)
    anywhere = pl.BlockSpec(memory_space=pl.ANY)
    table_rows = text_table.shape[0] + code_tables.shape[0]
    return pl.pallas_call(
        front_kernel,
        out_shape=(
            jax.ShapeDtypeStruct((frames * 8, width), BF16),
            jax.ShapeDtypeStruct((frames * 8, hidden_width), BF16),
            jax.ShapeDtypeStruct((frames * 8, hidden_width), BF16),
            jax.ShapeDtypeStruct((8, width // 8), F32),
            jax.ShapeDtypeStruct((frames, width), BF16),
            jax.ShapeDtypeStruct((8, frames * 8, 128), BF16),
        ),
        in_specs=[pl.BlockSpec(memory_space=pltpu.SMEM), anywhere, anywhere, vmem, vmem, vmem]
        + [anywhere] * 4,
        out_specs=(anywhere, anywhere, anywhere, vmem, vmem, vmem),
        scratch_shapes=[
            f32(table_rows, 128), bf(6, 2048, 128), dma(6), f32(rows, 128),
            bf(4, 2, frames, width), bf(2, frames, width), bf(2, frames, width), bf(2, frames, width),
            bf(2, frames, width), bf(frames, width), f32(frames, width),
            bf(8, frames * 8, 128), bf(8, frames * 8, 128), bf(8, frames * 8, 128),
            bf(width, hidden_width), bf(width, hidden_width),
            bf(frames * 8, hidden_width), bf(frames * 8, width), dma(4),
            bf(2, rows, width), bf(2, rows, hidden_width), bf(2, rows, hidden_width), dma(2, 3),
            f32(rows, width), f32(rows, 128), f32(rows, width), f32(frames, width), f32(8, width),
            dma(128), dma(128),
        ],
        compiler_params=pltpu.CompilerParams(
            collective_id=2, has_side_effects=True, vmem_limit_bytes=VMEM_LIMIT
        ),
        cost_estimate=pl.CostEstimate(
            flops=19_000_000_000, bytes_accessed=40_000_000, transcendentals=2_000_000
        ),
        name="front",
    )(ids, text_table, code_tables, temporal, context_weight, gain, gate_weight, up_weight, hidden, stream)


CHUNKS = 3


def total_of(refs):
    total = refs[0][...].astype(F32)
    for ref in refs[1:]:
        total = total + ref[...].astype(F32)
    return total


def add_into(out, refs):
    out[...] = total_of(refs).astype(BF16)


def reduce_kernel(
    normed, gate_back, up_back, gain, tables,
    weight_out, gain_out, table_mine, table_last,
    left_in, gate_in, up_in, turned, term, pair,
    x_bufs, x_sums, xz_bufs, z_bufs, z_sums, zx_bufs, y_term, y_bufs,
    own, other, t_bufs, t_sum, t_relay, gain_own, gain_in,
    local_sems, send_sems, recv_sems,
):
    core, x, y, z = position()
    quarter = term.shape[-1] // 4
    table_rows = own.shape[2]
    chunk_rows = table_rows // CHUNKS
    half_rows = chunk_rows // 2
    z_hi = lax.div(z, 2)
    sibling = device_at(1 - core, x, y, z)
    x_device = lambda at: device_at(core, at, y, z)
    y_device = lambda at: device_at(core, x, at, z)
    z_device = lambda at: device_at(core, x, y, at)
    t_rows = lambda c: pl.ds(c * chunk_rows, chunk_rows)
    keeps = [
        pltpu.make_async_copy(tables.at[core, :, :, t_rows(c)], own.at[:, :, t_rows(c)], local_sems.at[c])
        for c in range(CHUNKS)
    ]
    loads = [
        pltpu.make_async_copy(source, target, local_sems.at[CHUNKS + n])
        for n, (source, target) in enumerate(
            ((normed, left_in), (gate_back, gate_in), (up_back, up_in))
        )
    ]
    for load in loads + keeps:
        load.start()
    partners = (
        [sibling]
        + [x_device(step_to(x, by)) for by in (1, 2, 3)]
        + [y_device(step_to(y, by)) for by in (1, 2, 3)]
        + [z_device(step_to(z, by)) for by in (1, 2, 3)]
    )
    greet(partners)
    greeted(partners)
    copies = Copies(send_sems, recv_sems)

    def send_tables(c):
        return [
            copies.send(tables.at[1 - core, i, :, t_rows(c)], other.at[i, :, t_rows(c)], sibling)
            for i in range(4)
        ]

    gain_own[0] = gain[...]
    gain_copy = copies.send(gain_own.at[0], gain_in.at[0], sibling)
    table_pairs = [send_tables(c) for c in range(CHUNKS)]

    def make_term(q):
        turned[:128] = left_in[:, q * 128 : (q + 1) * 128].T
        turned[128:] = left_in[:, (q + 4) * 128 : (q + 5) * 128].T

        def body(i, carry):
            columns = pl.ds(pl.multiple_of(i * 256, 256), 256)
            left = turned[...]
            gate = jnp.dot(left, gate_in[:, columns], preferred_element_type=F32)
            up = jnp.dot(left, up_in[:, columns], preferred_element_type=F32)
            both = jnp.concatenate([gate.reshape(32, 8, 256), up.reshape(32, 8, 256)], axis=1)
            both = both.astype(BF16).reshape(2, 2, 4, 2, 16, 256)
            for hi in range(2):
                term[:, q, :, pl.ds(hi * 2, 2), :, columns] = both[hi]
            return carry

        lax.fori_loop(0, gate_in.shape[1] // 256, body, 0)

    pair_copies = []

    def send_pair(q):
        pair_copies.append(copies.send(term.at[1 - core, q], pair.at[q], sibling))

    def add_pair(q):
        pair_copies[q].wait_recv()

        def body(i, carry):
            column, depth = lax.div(i, 4), lax.rem(i, 4)
            total = term[core, q, column, depth].astype(F32) + pair[q, column, depth].astype(F32)
            term[core, q, column, depth] = total.astype(BF16)
            return carry

        lax.fori_loop(0, 16, body, 0)

    x_half = lambda half: pl.ds(half * quarter, quarter)
    z_half = lambda half: pl.ds((half + 2) * quarter, quarter)

    def make_ring(here, device, part, bufs, q):
        picks = [
            lambda half, n=n: bufs.at[(n, q) + (slice(None),) * (len(bufs.shape) - 3) + (x_half(half),)]
            for n in range(3)
        ]
        return Ring(copies, here, device, part, *picks)

    first_rings = [
        (
            make_ring(x, x_device, lambda at, half, q=q: term.at[core, q, at, :, :, x_half(half)], x_bufs, q),
            make_ring(z, z_device, lambda at, half, q=q: term.at[core, q, :, at, :, z_half(half)], z_bufs, q),
        )
        for q in range(4)
    ]
    second_rings = [
        (
            make_ring(z, z_device, lambda at, half, q=q: x_sums.at[q, at, :, x_half(half)], xz_bufs, q),
            make_ring(x, x_device, lambda at, half, q=q: z_sums.at[q, at, :, x_half(half)], zx_bufs, q),
        )
        for q in range(4)
    ]

    def first_out(q):
        first_rings[q][0].third(add_into, lambda half: x_sums.at[q, :, :, x_half(half)])
        first_rings[q][1].third(add_into, lambda half: z_sums.at[q, :, :, x_half(half)])
        for ring in second_rings[q]:
            ring.first()

    def second_out(q):
        second_rings[q][0].third(add_into, lambda half: y_term.at[q, :, x_half(half)])
        second_rings[q][1].third(add_into, lambda half: y_term.at[q, :, z_half(half)])

    def first_start(q):
        add_pair(q)
        for ring in first_rings[q]:
            ring.first()

    def first_middle(q):
        for ring in first_rings[q]:
            ring.second(add_into)

    def second_middle(q):
        for ring in second_rings[q]:
            ring.second(add_into)

    t_half = lambda c, half: pl.ds(c * chunk_rows + half * half_rows, half_rows)
    t_rings = [
        Ring(
            copies, y, y_device,
            lambda at, half, c=c: own.at[at, :, t_half(c, half)],
            *(lambda half, n=n, c=c: t_bufs.at[n, :, t_half(c, half)] for n in range(3)),
        )
        for c in range(CHUNKS)
    ]

    def add_tables(out, refs):
        def body(i, carry):
            rows = pl.ds(pl.multiple_of(i * 64, 64), 64)
            for hi in range(2):
                out[hi, rows] = total_of([ref.at[hi, rows] for ref in refs]).astype(BF16)
            return carry

        lax.fori_loop(0, half_rows // 64, body, 0)

    def pair_tables(c):
        keeps[c].wait()
        for copy in table_pairs[c]:
            copy.wait_recv()

        def body(i, carry):
            rows = pl.ds(pl.multiple_of(c * chunk_rows + lax.rem(i, chunk_rows // 128) * 128, 128), 128)
            at = lax.div(i, chunk_rows // 128)
            for hi in range(2):
                own[at, hi, rows] = total_of([own.at[at, hi, rows], other.at[at, hi, rows]]).astype(BF16)
            return carry

        lax.fori_loop(0, 4 * (chunk_rows // 128), body, 0)
        t_rings[c].first()

    t_relays, t_arrivals = {}, []

    def tables_out(c):
        t_rings[c].third(add_tables, lambda half: t_sum.at[:, t_half(c, half)])
        t_relays[c] = [
            copies.send(t_sum.at[1 - z_hi, t_half(c, half)], t_relay.at[t_half(c, half)], z_device(step_to(z, by)))
            for half, by in ((0, 1), (1, 3))
        ]

    def tables_relay(c):
        for copy, half, by in zip(t_relays[c], (0, 1), (1, 3)):
            copy.wait_recv()
            rows = t_half(c, half)
            t_arrivals.append(copies.send(t_relay.at[rows], table_last.at[rows], z_device(step_to(z, by))))

    def gain_round(index, device, here):
        gain_own[index] = gain_own[index - 1] + gain_sum
        return [
            copies.send(gain_own.at[index], gain_in.at[index * 3 + by - 3], device(step_to(here, by)))
            for by in (1, 2, 3)
        ]

    def gain_total(waited, slots):
        for copy in waited:
            copy.wait_recv()
        total = gain_in[slots[0]]
        for slot in slots[1:]:
            total = total + gain_in[slot]
        return total

    pair_tables(0)
    for load in loads:
        load.wait()
    make_term(0)
    send_pair(0)
    gain_sum = gain_total([gain_copy], [0])
    gain_copies = gain_round(1, x_device, x)
    pair_tables(1)
    pair_tables(2)
    make_term(1)
    send_pair(1)
    gain_sum = gain_total(gain_copies, [1, 2, 3])
    gain_copies = gain_round(2, z_device, z)
    first_start(0)
    t_rings[0].second(add_tables)
    make_term(2)
    send_pair(2)
    gain_sum = gain_total(gain_copies, [4, 5, 6])
    gain_copies = gain_round(3, y_device, y)
    first_start(1)
    first_middle(0)
    make_term(3)
    send_pair(3)
    t_rings[1].second(add_tables)
    first_start(2)
    first_middle(1)
    first_out(0)
    t_rings[2].second(add_tables)
    first_start(3)
    first_middle(2)
    first_out(1)
    second_middle(0)
    tables_out(0)
    first_middle(3)
    first_out(2)
    second_middle(1)
    second_out(0)
    tables_out(1)
    tables_relay(0)
    first_out(3)
    second_middle(2)
    second_out(1)
    tables_out(2)
    tables_relay(1)
    second_middle(3)
    second_out(2)
    second_out(3)

    y_half = lambda half: pl.ds(half * 2 * quarter, 2 * quarter)
    y_ring = Ring(
        copies, y, y_device,
        lambda at, half: y_term.at[at, :, y_half(half)],
        *(lambda half, n=n: y_bufs.at[n, :, y_half(half)] for n in range(3)),
    )
    y_ring.first()
    tables_relay(2)
    gain_out[...] = gain_own[3] + gain_total(gain_copies, [7, 8, 9])
    y_ring.second(add_into)

    def copy_mine(i, carry):
        rows = pl.ds(pl.multiple_of(i * 128, 128), 128)
        table_mine[rows] = t_sum[z_hi, rows]
        return carry

    lax.fori_loop(0, table_rows // 128, copy_mine, 0)

    def finish_weights(out, refs):
        weight_out[:, out] = total_of(refs)

    y_ring.third(finish_weights, y_half)
    for copy in t_arrivals:
        copy.wait_recv()
    copies.finish()


def reduce_all(normed, gate_back, up_back, gain_part, tables):
    rows, features = normed.shape
    width = gate_back.shape[1]
    table_rows = tables.shape[3]
    bf = lambda *shape: pltpu.VMEM(shape, BF16)
    vmem = pl.BlockSpec(memory_space=pltpu.VMEM)
    anywhere = pl.BlockSpec(memory_space=pl.ANY)
    return pl.pallas_call(
        reduce_kernel,
        out_shape=(
            jax.ShapeDtypeStruct((16, width), F32),
            jax.ShapeDtypeStruct((8, 128), F32),
            jax.ShapeDtypeStruct((table_rows, 128), BF16),
            jax.ShapeDtypeStruct((table_rows, 128), BF16),
        ),
        in_specs=[anywhere, anywhere, anywhere, vmem, anywhere],
        out_specs=(vmem,) * 4,
        scratch_shapes=[
            bf(rows, features), bf(rows, width), bf(rows, width), bf(256, rows),
            bf(2, 4, 4, 4, 16, width), bf(4, 4, 4, 16, width),
            bf(3, 4, 4, 16, width // 2), bf(4, 4, 16, width // 2), bf(3, 4, 16, width // 2),
            bf(3, 4, 4, 16, width // 2), bf(4, 4, 16, width // 2), bf(3, 4, 16, width // 2),
            bf(4, 16, width), bf(3, 16, width),
            bf(4, 2, table_rows, 128), bf(4, 2, table_rows, 128), bf(3, 2, table_rows, 128),
            bf(2, table_rows, 128), bf(table_rows, 128),
            pltpu.VMEM((4, 8, 128), F32), pltpu.VMEM((10, 8, 128), F32),
            pltpu.SemaphoreType.DMA((CHUNKS + 3,)),
            pltpu.SemaphoreType.DMA((160,)),
            pltpu.SemaphoreType.DMA((160,)),
        ],
        compiler_params=pltpu.CompilerParams(
            collective_id=1, has_side_effects=True, vmem_limit_bytes=VMEM_LIMIT
        ),
        cost_estimate=pl.CostEstimate(flops=9_000_000_000, bytes_accessed=20_000_000, transcendentals=0),
        name="reduce_all",
    )(normed, gate_back, up_back, gain_part, tables)


def results_kernel(weights, mine, last, gate_out, up_out, text_out, code_out):
    gate_out[...] = weights[:8]
    up_out[...] = weights[8:]
    text_rows = text_out.shape[0]

    def text_body(i, carry):
        rows = pl.ds(pl.multiple_of(i * 128, 128), 128)
        text_out[rows] = mine[rows].astype(F32) + last[rows].astype(F32)
        return carry

    lax.fori_loop(0, text_rows // 128, text_body, 0)
    for c in range(code_out.shape[0]):
        rows = pl.ds(text_rows + c * code_out.shape[1], code_out.shape[1])
        code_out[c] = mine[rows].astype(F32) + last[rows].astype(F32)


def results(weights, mine, last, text_rows, codes):
    vmem = pl.BlockSpec(memory_space=pltpu.VMEM)
    code_rows = (mine.shape[0] - text_rows) // codes
    return pl.pallas_call(
        results_kernel,
        out_shape=(
            jax.ShapeDtypeStruct((8, weights.shape[1]), F32),
            jax.ShapeDtypeStruct((8, weights.shape[1]), F32),
            jax.ShapeDtypeStruct((text_rows, 128), F32),
            jax.ShapeDtypeStruct((codes, code_rows, 128), F32),
        ),
        in_specs=[vmem] * 3,
        out_specs=(vmem,) * 4,
        compiler_params=pltpu.CompilerParams(vmem_limit_bytes=VMEM_LIMIT),
        name="results",
    )(weights, mine, last)


def scatter_kernel(ids, grads, tables, rows, total, text_count, card, codes):
    frames = grads.shape[0]
    count = total.shape[0]

    def clear(i, carry):
        total[pl.ds(pl.multiple_of(i * 256, 256), 256)] = jnp.zeros((256, 128), F32)
        return carry

    lax.fori_loop(0, count // 256, clear, 0)

    def widen(i, carry):
        block = grads[pl.ds(i * 16, 16)].astype(F32).reshape(128, 128)
        rows[pl.ds(pl.multiple_of(i * 128, 128), 128)] = block
        return carry

    lax.fori_loop(0, frames // 16, widen, 0)

    def body(f, carry):
        places = [ids[k * frames + f] for k in range(codes + 1)]
        sums = [
            total[pl.ds(places[k], 1)] + rows[pl.ds(f * (codes + 1) + k, 1)]
            for k in range(codes + 1)
        ]
        for k in range(codes + 1):
            total[pl.ds(places[k], 1)] = sums[k]
        return carry

    lax.fori_loop(0, frames, body, 0, unroll=4)

    text_block, code_block = text_count // 16, card // 16
    for block in range(16):
        z_hi, y, core = block // 8, block // 2 % 4, block % 2
        tables[core, y, z_hi, :text_block] = total[
            block * text_block : (block + 1) * text_block
        ].astype(BF16)
        for c in range(codes):
            first = text_count + c * card + block * code_block
            tables[core, y, z_hi, pl.ds(text_block + c * code_block, code_block)] = total[
                first : first + code_block
            ].astype(BF16)


def scatter_rows(ids, grads, text_count, card, codes):
    rows = text_count // 16 + codes * card // 16
    return pl.pallas_call(
        functools.partial(scatter_kernel, text_count=text_count, card=card, codes=codes),
        out_shape=jax.ShapeDtypeStruct((2, 4, 2, rows, 128), BF16),
        in_specs=[pl.BlockSpec(memory_space=pltpu.SMEM), pl.BlockSpec(memory_space=pltpu.VMEM)],
        out_specs=pl.BlockSpec(memory_space=pltpu.VMEM),
        scratch_shapes=[
            pltpu.VMEM((grads.shape[0] * (codes + 1), 128), F32),
            pltpu.VMEM((text_count + codes * card, 128), F32),
        ],
        compiler_params=pltpu.CompilerParams(vmem_limit_bytes=VMEM_LIMIT),
        name="scatter_rows",
    )(ids, grads)


def on_device(
    temporal_out,
    context_weight,
    text_ids,
    code_ids,
    text_table,
    code_tables,
    norm_gain,
    gate_weight,
    up_weight,
    hidden_grad,
    stream_grad,
):
    code_count, card_size, feature_width = code_tables.shape
    text_count = text_table.shape[0]
    code_offsets = jnp.arange(code_count, dtype=jnp.int32)[:, None] * card_size + text_count
    places = jnp.concatenate([text_ids[None], code_ids.T + code_offsets], axis=0).reshape(-1)
    normed, gate_back, up_back, gain_part, context_grad, grid = front(
        places,
        text_table,
        code_tables.reshape(code_count * card_size, feature_width),
        temporal_out,
        context_weight,
        norm_gain.reshape(1, -1),
        gate_weight,
        up_weight,
        hidden_grad.reshape(-1, hidden_grad.shape[2]),
        stream_grad.reshape(-1, stream_grad.shape[2]),
    )
    tables = scatter_rows(places, grid.reshape(-1, 8, feature_width), text_count, card_size, code_count)
    weights, gain_sum, mine, last = reduce_all(normed, gate_back, up_back, gain_part, tables)
    gate_grad, up_grad, text_grad, code_grad = results(
        weights, mine, last, text_count // lax.axis_size("seq"), code_count
    )
    own_place = lax.axis_index("seq") * lax.axis_size("tp") + lax.axis_index("tp")
    gain_grad = lax.dynamic_slice_in_dim(gain_sum.reshape(-1), own_place * 8, 8)
    return (gate_grad, up_grad, gain_grad, text_grad, code_grad, context_grad)


def solution(mesh):
    return jax.shard_map(
        on_device,
        mesh=mesh,
        in_specs=(
            P("seq", "tp"),
            P("tp", None),
            P("seq"),
            P("seq", None),
            P(None, "tp"),
            P(None, None, "tp"),
            P(),
            P(),
            P(),
            P(("seq", "tp"), None, None),
            P(("seq", "tp"), None, None),
        ),
        out_specs=(
            P(("seq", "tp"), None),
            P(("seq", "tp"), None),
            P(("seq", "tp")),
            P("seq", "tp"),
            P(None, "seq", "tp"),
            P(("seq", "tp"), None),
        ),
        check_vma=False,
    )
```

```python
import functools

import jax
import jax.numpy as jnp
from jax import lax
from jax.experimental import pallas as pl
from jax.experimental.pallas import tpu as pltpu
from jax.sharding import PartitionSpec as P

EPSILON = 1e-05

MESH = pl.DeviceIdType.MESH
F32 = jnp.float32
BF16 = jnp.bfloat16
VMEM_LIMIT = 60 * 1024 * 1024


def position():
    seq = lax.axis_index("seq")
    tp = lax.axis_index("tp")
    core = lax.rem(seq, 2)
    y = lax.rem(lax.div(seq, 2), 4)
    z_hi = lax.div(seq, 8)
    x = lax.div(tp, 2)
    z_lo = lax.rem(tp, 2)
    return core, x, y, z_hi * 2 + z_lo


def device_at(core, x, y, z):
    seq = (lax.div(z, 2) * 4 + y) * 2 + core
    tp = x * 2 + lax.rem(z, 2)
    return (seq, tp)


def step_to(value, by):
    return lax.rem(value + by, 4)


def greet(devices):
    for device in devices:
        pl.semaphore_signal(
            pltpu.get_barrier_semaphore(), inc=1, device_id=device, device_id_type=MESH
        )


def greeted(devices):
    pl.semaphore_wait(pltpu.get_barrier_semaphore(), len(devices))


class Copies:
    def __init__(self, send_sems, recv_sems):
        self.send_sems, self.recv_sems, self.made = send_sems, recv_sems, []

    def send(self, source, target, device):
        at = len(self.made)
        copy = pltpu.make_async_remote_copy(
            src_ref=source,
            dst_ref=target,
            send_sem=self.send_sems.at[at],
            recv_sem=self.recv_sems.at[at],
            device_id=device,
            device_id_type=MESH,
        )
        copy.start()
        self.made.append(copy)
        return copy

    def finish(self):
        for copy in self.made:
            copy.wait_send()


class Ring:
    def __init__(self, copies, here, device, part, pass_on, direct, ended):
        self.copies, self.here, self.device, self.part = copies, here, device, part
        self.pass_on, self.direct, self.ended = pass_on, direct, ended

    def first(self):
        for by in (2, 1, 3):
            self.first_to(by)

    def first_to(self, by):
        there = step_to(self.here, by)
        up_device, down_device = (self.device(step_to(self.here, to)) for to in (1, 3))
        send = self.copies.send
        if by == 2:
            self.from_down = send(self.part(there, 0), self.pass_on(0), up_device)
            self.from_up = send(self.part(there, 1), self.pass_on(1), down_device)
        elif by == 1:
            self.near = [send(self.part(there, 1), self.direct(1), up_device)]
        else:
            self.near.append(send(self.part(there, 0), self.direct(0), down_device))

    def second(self, add):
        up, down = step_to(self.here, 1), step_to(self.here, 3)
        self.from_down.wait_recv()
        add(self.part(up, 0), [self.part(up, 0), self.pass_on(0)])
        last_up = self.copies.send(self.part(up, 0), self.ended(0), self.device(up))
        self.from_up.wait_recv()
        add(self.part(down, 1), [self.part(down, 1), self.pass_on(1)])
        last_down = self.copies.send(self.part(down, 1), self.ended(1), self.device(down))
        self.last = [last_up, last_down]

    def third(self, add, out):
        for copy in self.near + self.last:
            copy.wait_recv()
        for half in (0, 1):
            add(out(half), [self.part(self.here, half), self.direct(half), self.ended(half)])


class Exchange:
    def __init__(self, copies, x, z_lo, device, chunk, landing):
        self.copies, self.x, self.z_lo, self.device = copies, x, z_lo, device
        self.chunk, self.landing, self.arrivals = chunk, landing, []

    def place(self, by_x, by_z):
        z_lo = self.z_lo if by_z == 0 else 1 - self.z_lo
        return step_to(self.x, by_x) * 2 + z_lo

    def start(self, by_x, by_z):
        own, there = self.place(0, 0), self.place(by_x, by_z)
        self.arrivals.append(
            self.copies.send(self.chunk(there), self.landing(own), self.device(there))
        )

    def arrive(self):
        for copy in self.arrivals:
            copy.wait_recv()


ORDER = ((2, 1), (2, 0), (1, 1), (3, 1), (1, 0), (3, 0), (0, 1), (0, 0))
TILES = 4


def front_kernel(
    ids, text_table, code_tables, temporal, context_weight, gain, gate_weight, up_weight, hidden, stream,
    normed_out, gate_out, up_out, gain_out, context_out, grid_out,
    table, staged, table_sems, picked,
    c_term, c_pass, c_direct, c_ended, c_pair, c_last, context,
    e_send, e_in, g_send,
    gate_w, up_w, hidden_in, stream_in, load_sems,
    normed, gate_back, up_back, out_sems, unit, scale, back, context_grad, gain_sum, send_sems, recv_sems,
):
    core, x, y, z = position()
    z_lo = lax.rem(z, 2)
    own = x * 2 + z_lo
    frames_all = temporal.shape[0]
    frames = frames_all // 8
    tile = frames // TILES
    rows = tile * 8
    seq = lax.axis_index("seq")
    device = lambda place: (seq, place)
    copies = Copies(send_sems, recv_sems)

    loads = []
    for at, (source, target) in enumerate(
        ((gate_weight, gate_w), (up_weight, up_w), (hidden, hidden_in), (stream, stream_in))
    ):
        loads.append(pltpu.make_async_copy(source, target, load_sems.at[at]))

    block = staged.shape[1]
    text_blocks = text_table.shape[0] // block
    blocks = table.shape[0] // block
    depth = staged.shape[0]

    def load_block(i):
        source = text_table if i < text_blocks else code_tables
        first = (i if i < text_blocks else i - text_blocks) * block
        return pltpu.make_async_copy(
            source.at[pl.ds(first, block)], staged.at[i % depth], table_sems.at[i % depth]
        )

    block_loads = [load_block(i) for i in range(blocks)]
    for i in range(depth):
        block_loads[i].start()
    others = [device(lax.rem(own + by, 8)) for by in range(1, 8)]
    greet(others)

    def context_part(at):
        def body(low, carry):
            block_rows = pl.ds(pl.multiple_of((at * 2 + low) * frames, frames), frames)
            partial = jnp.dot(temporal[block_rows], context_weight[...], preferred_element_type=F32)
            c_term[at, low] = partial.astype(BF16)
            return carry

        lax.fori_loop(0, 2, body, 0)

    half_width = c_term.shape[-1] // 2
    half_frames = frames // 2
    c_half = lambda half: pl.ds(half * half_width, half_width)
    c_frames = [pl.ds(h * half_frames, half_frames) for h in range(2)]

    def context_ring(h):
        pick = lambda ref: lambda half: ref.at[:, c_frames[h], c_half(half)]
        return Ring(
            copies, x, lambda at: device(at * 2 + z_lo),
            lambda at, half: c_term.at[at, :, c_frames[h], c_half(half)],
            pick(c_pass), pick(c_direct), pick(c_ended),
        )

    c_rings = [context_ring(h) for h in range(2)]

    def add_context(out, refs):
        def body(i, carry):
            at = pl.ds(pl.multiple_of(lax.rem(i, half_frames // 16) * 16, 16), 16)
            low = lax.div(i, half_frames // 16)
            out[low, at] = total_of([ref.at[low, at] for ref in refs]).astype(BF16)
            return carry

        lax.fori_loop(0, frames // 16, body, 0)

    def context_pair(h):
        c_rings[h].third(add_context, lambda half: c_pair.at[:, c_frames[h], c_half(half)])
        there = device(x * 2 + 1 - z_lo)
        return copies.send(c_pair.at[1 - z_lo, c_frames[h]], c_last.at[c_frames[h]], there)

    def context_total(h, copy):
        copy.wait_recv()

        def body(i, carry):
            at = pl.ds(pl.multiple_of(h * half_frames + i * 16, 16), 16)
            context[at] = total_of([c_pair.at[z_lo, at], c_last.at[at]])
            return carry

        lax.fori_loop(0, half_frames // 16, body, 0)

    context_part(step_to(x, 2))
    greeted(others)
    for by in (2, 1, 3):
        c_rings[0].first_to(by)
        context_part(step_to(x, {2: 1, 1: 3, 3: 0}[by]))

    for i in range(blocks):
        block_loads[i].wait()

        def widen(j, carry):
            at = pl.multiple_of(j * 128, 128)
            table[pl.ds(i * block + at, 128)] = staged[i % depth, pl.ds(at, 128)].astype(F32)
            return carry

        lax.fori_loop(0, block // 128, widen, 0)
        if i + depth < blocks:
            block_loads[i + depth].start()
        if i == blocks - depth:
            for load in loads:
                load.start()

    def gather(t, place, target):
        def body(f, carry):
            frame = place * frames + t * tile + f
            for k in range(8):
                picked[pl.ds(f * 8 + k, 1)] = table[pl.ds(ids[k * frames_all + frame], 1)]
            return carry

        lax.fori_loop(0, tile, body, 0, unroll=16)
        target[...] = picked[...].astype(BF16)

    def tile_rows(t):
        return pl.ds(t * rows, rows)

    def exchange(t, send_ref, in_ref):
        return Exchange(
            copies, x, z_lo, device,
            lambda place: send_ref.at[place, tile_rows(t)],
            lambda place: in_ref.at[place, tile_rows(t)],
        )

    rows_in = [exchange(t, e_send, e_in) for t in range(TILES)]
    rows_back = [exchange(t, g_send, grid_out) for t in range(TILES)]

    def gather_tile(t):
        for by_x, by_z in ORDER:
            place = rows_in[t].place(by_x, by_z)
            if (by_x, by_z) == (0, 0):
                gather(t, place, e_in.at[place, tile_rows(t)])
            else:
                gather(t, place, e_send.at[place, tile_rows(t)])

    def send_tile(t):
        for by_x, by_z in ORDER[:-1]:
            rows_in[t].start(by_x, by_z)

    gather_tile(0)
    c_rings[0].second(add_context)
    send_tile(0)
    c_rings[1].first()
    gather_tile(1)
    c_copy = context_pair(0)
    send_tile(1)
    gather_tile(2)
    c_rings[1].second(add_context)
    send_tile(2)
    gather_tile(3)
    context_total(0, c_copy)

    width = context.shape[1]
    column_blocks = width // 128
    gain_sum[...] = jnp.zeros(gain_sum.shape, F32)
    for load in loads:
        load.wait()

    def run_tile(t):
        slot = t % 2
        rows_in[t].arrive()

        def norm(i, carry):
            first = t * rows + i * 32
            at = pl.ds(pl.multiple_of(i * 32, 32), 32)
            frame_rows = [
                context[pl.ds(t * tile + i * 4 + f, 1)] for f in range(4)
            ]
            spread = jnp.concatenate([jnp.broadcast_to(row, (8, width)) for row in frame_rows], axis=0)
            embedded = jnp.concatenate(
                [e_in[j, pl.ds(pl.multiple_of(first, 32), 32)] for j in range(column_blocks)], axis=1
            )
            depth = (spread + embedded.astype(F32)).astype(BF16).astype(F32)
            inv = lax.rsqrt(jnp.mean(depth * depth, axis=1, keepdims=True) + EPSILON)
            unit_rows = depth * inv
            unit[at] = unit_rows
            scale[at] = jnp.broadcast_to(inv, (32, 128))
            normed[slot, at] = (unit_rows * gain[...]).astype(BF16)
            return carry

        lax.fori_loop(0, rows // 32, norm, 0)

        def forward_pass(j, carry):
            columns = pl.ds(pl.multiple_of(j * 256, 256), 256)
            left = normed[slot]
            gate = jnp.dot(left, gate_w[:, columns], preferred_element_type=F32)
            up = jnp.dot(left, up_w[:, columns], preferred_element_type=F32)
            upstream = hidden_in[pl.ds(t * rows, rows), columns].astype(F32)
            sigma = jax.nn.sigmoid(gate)
            with_sigma = upstream * sigma
            gate_back[slot, :, columns] = (with_sigma * up * (1.0 + gate * (1.0 - sigma))).astype(BF16)
            up_back[slot, :, columns] = (with_sigma * gate).astype(BF16)
            return carry

        lax.fori_loop(0, gate_w.shape[1] // 256, forward_pass, 0)
        outs = [
            pltpu.make_async_copy(ref.at[slot], target.at[pl.ds(t * rows, rows)], out_sems.at[slot, n])
            for n, (ref, target) in enumerate(
                ((normed, normed_out), (gate_back, gate_out), (up_back, up_out))
            )
        ]
        for out in outs:
            out.start()

        transposed = (((1,), (1,)), ((), ()))

        def backward_pass(j, carry):
            columns = pl.ds(pl.multiple_of(j * 256, 256), 256)
            total = lax.dot_general(
                gate_back[slot], gate_w[columns], transposed, preferred_element_type=F32
            )
            total = total + lax.dot_general(
                up_back[slot], up_w[columns], transposed, preferred_element_type=F32
            )
            back[:, columns] = total
            return carry

        lax.fori_loop(0, width // 256, backward_pass, 0)

        def finish(i, carry):
            at = pl.ds(pl.multiple_of(i * 64, 64), 64)
            whole = pl.ds(pl.multiple_of(t * rows + i * 64, 64), 64)
            normed_back, unit_rows = back[at], unit[at]
            gain_sum[...] += jnp.sum((normed_back * unit_rows).reshape(8, 8, width), axis=0)
            scaled = normed_back * gain[...]
            mean = jnp.mean(scaled * unit_rows, axis=1, keepdims=True)
            depth = stream_in[whole].astype(F32) + scale[at, :1] * (scaled - unit_rows * mean)
            depth = depth.astype(BF16)
            for j in range(column_blocks):
                g_send[j, whole] = depth[:, j * 128 : (j + 1) * 128]
            frame_rows = pl.ds(pl.multiple_of(t * tile + i * 8, 8), 8)
            context_grad[frame_rows] = jnp.sum(depth.astype(F32).reshape(8, 8, width), axis=1)
            return carry

        lax.fori_loop(0, rows // 64, finish, 0)
        for by_x, by_z in ORDER[:-1]:
            rows_back[t].start(by_x, by_z)
        grid_out[own, pl.ds(t * rows, rows)] = g_send[own, pl.ds(t * rows, rows)]
        return outs

    outs = [run_tile(0)]
    c_copy = context_pair(1)
    send_tile(3)
    outs.append(run_tile(1))
    for out in outs[0]:
        out.wait()
    context_total(1, c_copy)
    outs.append(run_tile(2))
    for out in outs[1]:
        out.wait()
    outs.append(run_tile(3))
    context_out[...] = context_grad[...].astype(BF16)
    gain_row = jnp.sum(gain_sum[...], axis=0, keepdims=True)
    for j in range(8):
        gain_out[j : j + 1] = gain_row[:, j * 128 : (j + 1) * 128]
    for out in outs[2] + outs[3]:
        out.wait()
    for t in range(TILES):
        rows_back[t].arrive()
    copies.finish()


def front(ids, text_table, code_tables, temporal, context_weight, gain, gate_weight, up_weight, hidden, stream):
    frames_all = temporal.shape[0]
    frames = frames_all // 8
    width, hidden_width = gate_weight.shape
    rows = frames * 8 // TILES
    bf = lambda *shape: pltpu.VMEM(shape, BF16)
    f32 = lambda *shape: pltpu.VMEM(shape, F32)
    dma = lambda *shape: pltpu.SemaphoreType.DMA(shape)
    vmem = pl.BlockSpec(memory_space=pltpu.VMEM)
    anywhere = pl.BlockSpec(memory_space=pl.ANY)
    table_rows = text_table.shape[0] + code_tables.shape[0]
    return pl.pallas_call(
        front_kernel,
        out_shape=(
            jax.ShapeDtypeStruct((frames * 8, width), BF16),
            jax.ShapeDtypeStruct((frames * 8, hidden_width), BF16),
            jax.ShapeDtypeStruct((frames * 8, hidden_width), BF16),
            jax.ShapeDtypeStruct((8, width // 8), F32),
            jax.ShapeDtypeStruct((frames, width), BF16),
            jax.ShapeDtypeStruct((8, frames * 8, 128), BF16),
        ),
        in_specs=[pl.BlockSpec(memory_space=pltpu.SMEM), anywhere, anywhere, vmem, vmem, vmem]
        + [anywhere] * 4,
        out_specs=(anywhere, anywhere, anywhere, vmem, vmem, vmem),
        scratch_shapes=[
            f32(table_rows, 128), bf(6, 2048, 128), dma(6), f32(rows, 128),
            bf(4, 2, frames, width), bf(2, frames, width), bf(2, frames, width), bf(2, frames, width),
            bf(2, frames, width), bf(frames, width), f32(frames, width),
            bf(8, frames * 8, 128), bf(8, frames * 8, 128), bf(8, frames * 8, 128),
            bf(width, hidden_width), bf(width, hidden_width),
            bf(frames * 8, hidden_width), bf(frames * 8, width), dma(4),
            bf(2, rows, width), bf(2, rows, hidden_width), bf(2, rows, hidden_width), dma(2, 3),
            f32(rows, width), f32(rows, 128), f32(rows, width), f32(frames, width), f32(8, width),
            dma(128), dma(128),
        ],
        compiler_params=pltpu.CompilerParams(
            collective_id=2, has_side_effects=True, vmem_limit_bytes=VMEM_LIMIT
        ),
        cost_estimate=pl.CostEstimate(
            flops=19_000_000_000, bytes_accessed=40_000_000, transcendentals=2_000_000
        ),
        name="front",
    )(ids, text_table, code_tables, temporal, context_weight, gain, gate_weight, up_weight, hidden, stream)


CHUNKS = 3


def total_of(refs):
    total = refs[0][...].astype(F32)
    for ref in refs[1:]:
        total = total + ref[...].astype(F32)
    return total


def add_into(out, refs):
    out[...] = total_of(refs).astype(BF16)


def reduce_kernel(
    normed, gate_back, up_back, gain, tables,
    weight_out, gain_out, table_mine, table_last,
    left_in, gate_in, up_in, turned, term, pair,
    x_bufs, x_sums, xz_bufs, z_bufs, z_sums, zx_bufs, y_term, y_bufs,
    own, other, t_bufs, t_sum, t_relay, gain_own, gain_in,
    local_sems, send_sems, recv_sems,
):
    core, x, y, z = position()
    quarter = term.shape[-1] // 4
    table_rows = own.shape[2]
    chunk_rows = table_rows // CHUNKS
    half_rows = chunk_rows // 2
    z_hi = lax.div(z, 2)
    sibling = device_at(1 - core, x, y, z)
    x_device = lambda at: device_at(core, at, y, z)
    y_device = lambda at: device_at(core, x, at, z)
    z_device = lambda at: device_at(core, x, y, at)
    t_rows = lambda c: pl.ds(c * chunk_rows, chunk_rows)
    keeps = [
        pltpu.make_async_copy(tables.at[core, :, :, t_rows(c)], own.at[:, :, t_rows(c)], local_sems.at[c])
        for c in range(CHUNKS)
    ]
    loads = [
        pltpu.make_async_copy(source, target, local_sems.at[CHUNKS + n])
        for n, (source, target) in enumerate(
            ((normed, left_in), (gate_back, gate_in), (up_back, up_in))
        )
    ]
    for load in loads + keeps:
        load.start()
    partners = (
        [sibling]
        + [x_device(step_to(x, by)) for by in (1, 2, 3)]
        + [y_device(step_to(y, by)) for by in (1, 2, 3)]
        + [z_device(step_to(z, by)) for by in (1, 2, 3)]
    )
    greet(partners)
    greeted(partners)
    copies = Copies(send_sems, recv_sems)

    def send_tables(c):
        return [
            copies.send(tables.at[1 - core, i, :, t_rows(c)], other.at[i, :, t_rows(c)], sibling)
            for i in range(4)
        ]

    gain_own[0] = gain[...]
    gain_copy = copies.send(gain_own.at[0], gain_in.at[0], sibling)
    table_pairs = [send_tables(c) for c in range(CHUNKS)]

    def make_term(q):
        turned[:128] = left_in[:, q * 128 : (q + 1) * 128].T
        turned[128:] = left_in[:, (q + 4) * 128 : (q + 5) * 128].T

        def body(i, carry):
            columns = pl.ds(pl.multiple_of(i * 256, 256), 256)
            left = turned[...]
            gate = jnp.dot(left, gate_in[:, columns], preferred_element_type=F32)
            up = jnp.dot(left, up_in[:, columns], preferred_element_type=F32)
            both = jnp.concatenate([gate.reshape(32, 8, 256), up.reshape(32, 8, 256)], axis=1)
            both = both.astype(BF16).reshape(2, 2, 4, 2, 16, 256)
            for hi in range(2):
                term[:, q, :, pl.ds(hi * 2, 2), :, columns] = both[hi]
            return carry

        lax.fori_loop(0, gate_in.shape[1] // 256, body, 0)

    pair_copies = []

    def send_pair(q):
        pair_copies.append(copies.send(term.at[1 - core, q], pair.at[q], sibling))

    def add_pair(q):
        pair_copies[q].wait_recv()

        def body(i, carry):
            column, depth = lax.div(i, 4), lax.rem(i, 4)
            total = term[core, q, column, depth].astype(F32) + pair[q, column, depth].astype(F32)
            term[core, q, column, depth] = total.astype(BF16)
            return carry

        lax.fori_loop(0, 16, body, 0)

    x_half = lambda half: pl.ds(half * quarter, quarter)
    z_half = lambda half: pl.ds((half + 2) * quarter, quarter)

    def make_ring(here, device, part, bufs, q):
        picks = [
            lambda half, n=n: bufs.at[(n, q) + (slice(None),) * (len(bufs.shape) - 3) + (x_half(half),)]
            for n in range(3)
        ]
        return Ring(copies, here, device, part, *picks)

    first_rings = [
        (
            make_ring(x, x_device, lambda at, half, q=q: term.at[core, q, at, :, :, x_half(half)], x_bufs, q),
            make_ring(z, z_device, lambda at, half, q=q: term.at[core, q, :, at, :, z_half(half)], z_bufs, q),
        )
        for q in range(4)
    ]
    second_rings = [
        (
            make_ring(z, z_device, lambda at, half, q=q: x_sums.at[q, at, :, x_half(half)], xz_bufs, q),
            make_ring(x, x_device, lambda at, half, q=q: z_sums.at[q, at, :, x_half(half)], zx_bufs, q),
        )
        for q in range(4)
    ]

    def first_out(q):
        first_rings[q][0].third(add_into, lambda half: x_sums.at[q, :, :, x_half(half)])
        first_rings[q][1].third(add_into, lambda half: z_sums.at[q, :, :, x_half(half)])
        for ring in second_rings[q]:
            ring.first()

    def second_out(q):
        second_rings[q][0].third(add_into, lambda half: y_term.at[q, :, x_half(half)])
        second_rings[q][1].third(add_into, lambda half: y_term.at[q, :, z_half(half)])

    def first_start(q):
        add_pair(q)
        for ring in first_rings[q]:
            ring.first()

    def first_middle(q):
        for ring in first_rings[q]:
            ring.second(add_into)

    def second_middle(q):
        for ring in second_rings[q]:
            ring.second(add_into)

    t_half = lambda c, half: pl.ds(c * chunk_rows + half * half_rows, half_rows)
    t_rings = [
        Ring(
            copies, y, y_device,
            lambda at, half, c=c: own.at[at, :, t_half(c, half)],
            *(lambda half, n=n, c=c: t_bufs.at[n, :, t_half(c, half)] for n in range(3)),
        )
        for c in range(CHUNKS)
    ]

    def add_tables(out, refs):
        def body(i, carry):
            rows = pl.ds(pl.multiple_of(i * 64, 64), 64)
            for hi in range(2):
                out[hi, rows] = total_of([ref.at[hi, rows] for ref in refs]).astype(BF16)
            return carry

        lax.fori_loop(0, half_rows // 64, body, 0)

    def pair_tables(c):
        keeps[c].wait()
        for copy in table_pairs[c]:
            copy.wait_recv()

        def body(i, carry):
            rows = pl.ds(pl.multiple_of(c * chunk_rows + lax.rem(i, chunk_rows // 128) * 128, 128), 128)
            at = lax.div(i, chunk_rows // 128)
            for hi in range(2):
                own[at, hi, rows] = total_of([own.at[at, hi, rows], other.at[at, hi, rows]]).astype(BF16)
            return carry

        lax.fori_loop(0, 4 * (chunk_rows // 128), body, 0)
        t_rings[c].first()

    t_relays, t_arrivals = {}, []

    def tables_out(c):
        t_rings[c].third(add_tables, lambda half: t_sum.at[:, t_half(c, half)])
        t_relays[c] = [
            copies.send(t_sum.at[1 - z_hi, t_half(c, half)], t_relay.at[t_half(c, half)], z_device(step_to(z, by)))
            for half, by in ((0, 1), (1, 3))
        ]

    def tables_relay(c):
        for copy, half, by in zip(t_relays[c], (0, 1), (1, 3)):
            copy.wait_recv()
            rows = t_half(c, half)
            t_arrivals.append(copies.send(t_relay.at[rows], table_last.at[rows], z_device(step_to(z, by))))

    def gain_round(index, device, here):
        gain_own[index] = gain_own[index - 1] + gain_sum
        return [
            copies.send(gain_own.at[index], gain_in.at[index * 3 + by - 3], device(step_to(here, by)))
            for by in (1, 2, 3)
        ]

    def gain_total(waited, slots):
        for copy in waited:
            copy.wait_recv()
        total = gain_in[slots[0]]
        for slot in slots[1:]:
            total = total + gain_in[slot]
        return total

    pair_tables(0)
    pair_tables(1)
    for load in loads:
        load.wait()
    make_term(0)
    send_pair(0)
    gain_sum = gain_total([gain_copy], [0])
    gain_copies = gain_round(1, x_device, x)
    pair_tables(2)
    make_term(1)
    send_pair(1)
    gain_sum = gain_total(gain_copies, [1, 2, 3])
    gain_copies = gain_round(2, z_device, z)
    first_start(0)
    t_rings[0].second(add_tables)
    make_term(2)
    send_pair(2)
    gain_sum = gain_total(gain_copies, [4, 5, 6])
    gain_copies = gain_round(3, y_device, y)
    first_start(1)
    first_middle(0)
    t_rings[1].second(add_tables)
    make_term(3)
    send_pair(3)
    first_start(2)
    first_middle(1)
    first_out(0)
    t_rings[2].second(add_tables)
    first_start(3)
    first_middle(2)
    first_out(1)
    second_middle(0)
    tables_out(0)
    first_middle(3)
    first_out(2)
    second_middle(1)
    second_out(0)
    tables_out(1)
    tables_relay(0)
    first_out(3)
    second_middle(2)
    second_out(1)
    tables_out(2)
    tables_relay(1)
    second_middle(3)
    second_out(2)
    second_out(3)

    y_half = lambda half: pl.ds(half * 2 * quarter, 2 * quarter)
    y_ring = Ring(
        copies, y, y_device,
        lambda at, half: y_term.at[at, :, y_half(half)],
        *(lambda half, n=n: y_bufs.at[n, :, y_half(half)] for n in range(3)),
    )
    y_ring.first()
    tables_relay(2)
    gain_out[...] = gain_own[3] + gain_total(gain_copies, [7, 8, 9])
    y_ring.second(add_into)

    def copy_mine(i, carry):
        rows = pl.ds(pl.multiple_of(i * 128, 128), 128)
        table_mine[rows] = t_sum[z_hi, rows]
        return carry

    lax.fori_loop(0, table_rows // 128, copy_mine, 0)

    def finish_weights(out, refs):
        weight_out[:, out] = total_of(refs)

    y_ring.third(finish_weights, y_half)
    for copy in t_arrivals:
        copy.wait_recv()
    copies.finish()


def reduce_all(normed, gate_back, up_back, gain_part, tables):
    rows, features = normed.shape
    width = gate_back.shape[1]
    table_rows = tables.shape[3]
    bf = lambda *shape: pltpu.VMEM(shape, BF16)
    vmem = pl.BlockSpec(memory_space=pltpu.VMEM)
    anywhere = pl.BlockSpec(memory_space=pl.ANY)
    return pl.pallas_call(
        reduce_kernel,
        out_shape=(
            jax.ShapeDtypeStruct((16, width), F32),
            jax.ShapeDtypeStruct((8, 128), F32),
            jax.ShapeDtypeStruct((table_rows, 128), BF16),
            jax.ShapeDtypeStruct((table_rows, 128), BF16),
        ),
        in_specs=[anywhere, anywhere, anywhere, vmem, anywhere],
        out_specs=(vmem,) * 4,
        scratch_shapes=[
            bf(rows, features), bf(rows, width), bf(rows, width), bf(256, rows),
            bf(2, 4, 4, 4, 16, width), bf(4, 4, 4, 16, width),
            bf(3, 4, 4, 16, width // 2), bf(4, 4, 16, width // 2), bf(3, 4, 16, width // 2),
            bf(3, 4, 4, 16, width // 2), bf(4, 4, 16, width // 2), bf(3, 4, 16, width // 2),
            bf(4, 16, width), bf(3, 16, width),
            bf(4, 2, table_rows, 128), bf(4, 2, table_rows, 128), bf(3, 2, table_rows, 128),
            bf(2, table_rows, 128), bf(table_rows, 128),
            pltpu.VMEM((4, 8, 128), F32), pltpu.VMEM((10, 8, 128), F32),
            pltpu.SemaphoreType.DMA((CHUNKS + 3,)),
            pltpu.SemaphoreType.DMA((160,)),
            pltpu.SemaphoreType.DMA((160,)),
        ],
        compiler_params=pltpu.CompilerParams(
            collective_id=1, has_side_effects=True, vmem_limit_bytes=VMEM_LIMIT
        ),
        cost_estimate=pl.CostEstimate(flops=9_000_000_000, bytes_accessed=20_000_000, transcendentals=0),
        name="reduce_all",
    )(normed, gate_back, up_back, gain_part, tables)


def results_kernel(weights, mine, last, gate_out, up_out, text_out, code_out):
    gate_out[...] = weights[:8]
    up_out[...] = weights[8:]
    text_rows = text_out.shape[0]

    def text_body(i, carry):
        rows = pl.ds(pl.multiple_of(i * 128, 128), 128)
        text_out[rows] = mine[rows].astype(F32) + last[rows].astype(F32)
        return carry

    lax.fori_loop(0, text_rows // 128, text_body, 0)
    for c in range(code_out.shape[0]):
        rows = pl.ds(text_rows + c * code_out.shape[1], code_out.shape[1])
        code_out[c] = mine[rows].astype(F32) + last[rows].astype(F32)


def results(weights, mine, last, text_rows, codes):
    vmem = pl.BlockSpec(memory_space=pltpu.VMEM)
    code_rows = (mine.shape[0] - text_rows) // codes
    return pl.pallas_call(
        results_kernel,
        out_shape=(
            jax.ShapeDtypeStruct((8, weights.shape[1]), F32),
            jax.ShapeDtypeStruct((8, weights.shape[1]), F32),
            jax.ShapeDtypeStruct((text_rows, 128), F32),
            jax.ShapeDtypeStruct((codes, code_rows, 128), F32),
        ),
        in_specs=[vmem] * 3,
        out_specs=(vmem,) * 4,
        compiler_params=pltpu.CompilerParams(vmem_limit_bytes=VMEM_LIMIT),
        name="results",
    )(weights, mine, last)


def scatter_kernel(ids, grads, tables, rows, total, text_count, card, codes):
    frames = grads.shape[0]
    count = total.shape[0]

    def clear(i, carry):
        total[pl.ds(pl.multiple_of(i * 256, 256), 256)] = jnp.zeros((256, 128), F32)
        return carry

    lax.fori_loop(0, count // 256, clear, 0)

    def widen(i, carry):
        block = grads[pl.ds(i * 16, 16)].astype(F32).reshape(128, 128)
        rows[pl.ds(pl.multiple_of(i * 128, 128), 128)] = block
        return carry

    lax.fori_loop(0, frames // 16, widen, 0)

    def body(f, carry):
        places = [ids[k * frames + f] for k in range(codes + 1)]
        sums = [
            total[pl.ds(places[k], 1)] + rows[pl.ds(f * (codes + 1) + k, 1)]
            for k in range(codes + 1)
        ]
        for k in range(codes + 1):
            total[pl.ds(places[k], 1)] = sums[k]
        return carry

    lax.fori_loop(0, frames, body, 0, unroll=16)

    text_block, code_block = text_count // 16, card // 16
    for block in range(16):
        z_hi, y, core = block // 8, block // 2 % 4, block % 2
        tables[core, y, z_hi, :text_block] = total[
            block * text_block : (block + 1) * text_block
        ].astype(BF16)
        for c in range(codes):
            first = text_count + c * card + block * code_block
            tables[core, y, z_hi, pl.ds(text_block + c * code_block, code_block)] = total[
                first : first + code_block
            ].astype(BF16)


def scatter_rows(ids, grads, text_count, card, codes):
    rows = text_count // 16 + codes * card // 16
    return pl.pallas_call(
        functools.partial(scatter_kernel, text_count=text_count, card=card, codes=codes),
        out_shape=jax.ShapeDtypeStruct((2, 4, 2, rows, 128), BF16),
        in_specs=[pl.BlockSpec(memory_space=pltpu.SMEM), pl.BlockSpec(memory_space=pltpu.VMEM)],
        out_specs=pl.BlockSpec(memory_space=pltpu.VMEM),
        scratch_shapes=[
            pltpu.VMEM((grads.shape[0] * (codes + 1), 128), F32),
            pltpu.VMEM((text_count + codes * card, 128), F32),
        ],
        compiler_params=pltpu.CompilerParams(vmem_limit_bytes=VMEM_LIMIT),
        name="scatter_rows",
    )(ids, grads)


def on_device(
    temporal_out,
    context_weight,
    text_ids,
    code_ids,
    text_table,
    code_tables,
    norm_gain,
    gate_weight,
    up_weight,
    hidden_grad,
    stream_grad,
):
    code_count, card_size, feature_width = code_tables.shape
    text_count = text_table.shape[0]
    code_offsets = jnp.arange(code_count, dtype=jnp.int32)[:, None] * card_size + text_count
    places = jnp.concatenate([text_ids[None], code_ids.T + code_offsets], axis=0).reshape(-1)
    normed, gate_back, up_back, gain_part, context_grad, grid = front(
        places,
        text_table,
        code_tables.reshape(code_count * card_size, feature_width),
        temporal_out,
        context_weight,
        norm_gain.reshape(1, -1),
        gate_weight,
        up_weight,
        hidden_grad.reshape(-1, hidden_grad.shape[2]),
        stream_grad.reshape(-1, stream_grad.shape[2]),
    )
    tables = scatter_rows(places, grid.reshape(-1, 8, feature_width), text_count, card_size, code_count)
    weights, gain_sum, mine, last = reduce_all(normed, gate_back, up_back, gain_part, tables)
    gate_grad, up_grad, text_grad, code_grad = results(
        weights, mine, last, text_count // lax.axis_size("seq"), code_count
    )
    own_place = lax.axis_index("seq") * lax.axis_size("tp") + lax.axis_index("tp")
    gain_grad = lax.dynamic_slice_in_dim(gain_sum.reshape(-1), own_place * 8, 8)
    return (gate_grad, up_grad, gain_grad, text_grad, code_grad, context_grad)


def solution(mesh):
    return jax.shard_map(
        on_device,
        mesh=mesh,
        in_specs=(
            P("seq", "tp"),
            P("tp", None),
            P("seq"),
            P("seq", None),
            P(None, "tp"),
            P(None, None, "tp"),
            P(),
            P(),
            P(),
            P(("seq", "tp"), None, None),
            P(("seq", "tp"), None, None),
        ),
        out_specs=(
            P(("seq", "tp"), None),
            P(("seq", "tp"), None),
            P(("seq", "tp")),
            P("seq", "tp"),
            P(None, "seq", "tp"),
            P(("seq", "tp"), None),
        ),
        check_vma=False,
    )
```
